128 devices in a mesh: fsdp: 32 (over x, y, core), tensor: 4 (over z).
Axes of the slice: x: 4, y: 4, z: 4, core: 2. Of those that a mesh axis runs over, the one named last changes fastest.
Arguments:
- momentum: float32 [8192, 26624], P('fsdp', 'tensor'), may hold values from -150 to 150
- gradient: bfloat16 [8192, 26624], P('fsdp', 'tensor'), may hold values from -6 to 6
- right_prev: float32 [256, 26624], P('fsdp', 'tensor'), may hold values from -0.0390625 to 0.0390625
Outputs:
- new_momentum: float32 [8192, 26624], P('fsdp', 'tensor')
- right_next: float32 [256, 26624], P('fsdp', 'tensor')
- update: bfloat16 [8192, 26624], P('fsdp', 'tensor')
The draws below stay inside these ranges and needn't reach their ends.
All inputs are finite; a program needn't handle non-finite values.
Results may differ from the reference program's by a relative error of at most 0.0017.
Values sent between devices are 32-bit elements; how exact they have to be, the bound alone decides.
A program may use at most 128 MiB of HBM per device.

```python
import math
import jax
import jax.numpy as jnp
from jax import lax

M_ROWS = 8192
N_COLS = 26624
RANK = 256


def draw_momentum(key, part):
    key = jax.random.fold_in(key, 11)
    key_base, key_rows, key_cols = jax.random.split(key, 3)
    base = jnp.clip(jax.random.normal(key_base, (M_ROWS, N_COLS), jnp.float32), -5.0, 5.0)
    rising = 3.0
    row_pos = jnp.arange(M_ROWS, dtype=jnp.float32) / M_ROWS - 0.5
    col_pos = jnp.arange(N_COLS, dtype=jnp.float32) / N_COLS - 0.5
    row_scale = jnp.exp(jax.random.uniform(key_rows, (M_ROWS,), jnp.float32, math.log(0.3), math.log(3.0))) * rising ** row_pos
    col_scale = jnp.exp(jax.random.uniform(key_cols, (N_COLS,), jnp.float32, math.log(0.3), math.log(3.0))) * rising ** col_pos
    return base * row_scale[:, None] * col_scale[None, :]


def block_scale(own_key, extent, cuts, low, high):
    def one(axis_at, blocks):
        heights = jax.random.uniform(jax.random.fold_in(jax.random.fold_in(own_key, 6), axis_at), (blocks,), jnp.float32, low / len(cuts), high / len(cuts))
        return jnp.repeat(jnp.exp(heights), extent[axis_at] // blocks).reshape((-1,) + (1,) * (len(extent) - axis_at - 1))

    gain = one(*cuts[0])
    for cut in cuts[1:]:
        gain = gain * one(*cut)
    return gain


def noise(rng, extent, width, reach, cuts=(), kind=jnp.bfloat16):
    values = width * jax.random.normal(rng, extent, jnp.float32)
    if cuts:
        values = values * block_scale(rng, extent, cuts, -0.22, 0.18)
    return jnp.clip(values, -reach, reach).astype(kind)


def setup_inputs(seed: int = 0) -> dict:
    splits = jax.random.split(jax.random.key(seed), 4)
    return {
        "momentum": draw_momentum(jax.random.fold_in(splits[3], 71), 0),
        "gradient": noise(splits[1], (M_ROWS, N_COLS), 1.0, 6.0, ((0, 32), (1, 4))),
        "right_prev": noise(splits[2], (RANK, N_COLS), N_COLS ** -0.5, 0.0390625, ((0, 32), (1, 4)), jnp.float32),
    }


def reference(momentum, gradient, right_prev):
    highest = lax.Precision.HIGHEST
    buffer = momentum + gradient.astype(jnp.float32)
    projected = lax.dot_general(buffer.astype(jnp.float32), right_prev.astype(jnp.float32), (((1,), (1,)), ((), ())), precision=highest, preferred_element_type=jnp.float32)
    gram_total = jnp.dot(projected.T.astype(jnp.float32), projected.astype(jnp.float32), precision=highest, preferred_element_type=jnp.float32)
    cholesky_low = jnp.linalg.cholesky(gram_total)
    orthonormal = jax.scipy.linalg.solve_triangular(cholesky_low, projected.T, lower=True).T
    right_full = jnp.dot(orthonormal.T.astype(jnp.float32), buffer.astype(jnp.float32), precision=highest, preferred_element_type=jnp.float32)
    col_norm = jnp.sqrt(lax.optimization_barrier(jnp.sum(right_full * right_full, axis=1))) + 1e-06
    right_next = right_full / col_norm[:, None]
    new_momentum = buffer - 0.05 * jnp.dot(orthonormal.astype(jnp.float32), right_full.astype(jnp.float32), precision=highest, preferred_element_type=jnp.float32)
    unit_scale = (M_ROWS * N_COLS / RANK) ** 0.5
    update = (unit_scale * jnp.dot(orthonormal.astype(jnp.float32), right_next.astype(jnp.float32), precision=highest, preferred_element_type=jnp.float32)).astype(jnp.bfloat16)
    return (new_momentum, right_next, update)
```

```python
import jax
import jax.numpy as jnp
from jax import lax
from jax.experimental import pallas as pl
from jax.experimental.pallas import tpu as pltpu
from jax.sharding import PartitionSpec as P

M_ROWS = 8192
N_COLS = 26624
RANK = 256
F32 = jnp.float32
BF16 = jnp.bfloat16
MESH = pl.DeviceIdType.MESH
HIGHEST = lax.Precision.HIGHEST

ROWS = 256
COLS = 6656
HALF = COLS // 2
STREAM = HALF // 2
PIECE = STREAM // 16
CUT = 56
CHUNK = 256
N_CHUNK = HALF // CHUNK
N_SEM = 176


def split(a):
    high = a.astype(BF16)
    return high, (a - high.astype(F32)).astype(BF16)


def dot(a, b, precision=None):
    return jnp.dot(a, b, precision=precision, preferred_element_type=F32)


def dot_nt(a, b, precision=None):
    return lax.dot_general(
        a, b, (((1,), (1,)), ((), ())), precision=precision, preferred_element_type=F32
    )


def dot_tn(a, b, precision=None):
    return lax.dot_general(
        a, b, (((0,), (0,)), ((), ())), precision=precision, preferred_element_type=F32
    )


def row_of(v, i):
    return jnp.broadcast_to(v[i : i + 1, :], v.shape)


def factor_panel(work, base, panel):
    first = base + 8 * panel
    sub = lax.broadcasted_iota(jnp.int32, (8, 128), 0)
    lane = lax.broadcasted_iota(jnp.int32, (8, 128), 1)
    rows = pl.ds(pl.multiple_of(first, 8), 8)
    parts = [work[rows, 128 * t : 128 * t + 128] for t in range(4)]
    here = pltpu.roll(parts[base // 128], lax.rem(128 - 8 * panel, 128), 1)
    cols = [jnp.broadcast_to(here[:, i : i + 1], (8, 128)) for i in range(8)]
    for i in range(8):
        inv = lax.rsqrt(row_of(cols[i], i))
        coef = jnp.where(sub > i, cols[i] * inv, 0.0)
        for t in range(4):
            scaled = row_of(parts[t], i) * inv
            parts[t] = jnp.where(sub == i, scaled, parts[t] - coef * scaled)
        for j in range(i + 1, 8):
            cols[j] = cols[j] - coef * (row_of(cols[j], i) * inv)
    for t in range(4):
        work[rows, 128 * t : 128 * t + 128] = parts[t]
    left = jnp.where(lane > 8 * panel + 7, parts[base // 128], 0.0)
    whole = jnp.concatenate(parts, axis=1)
    work[base : base + 128, :] = work[base : base + 128, :] - dot_tn(left, whole, HIGHEST)


def kernel(
    m_hbm, g_hbm, v_in, wt_out, lhs_out, m8_out,
    m_v, g_v, bts, btr, bh, bl, vb, pt, ptr, zr, pts, ph, plo,
    gx, gy, gg, wt, r1p, r1m, r2, r3, wown, work, sx, sy, sz, sc, q_s,
    ss, rs, ls,
):
    f = lax.axis_index("fsdp")
    z = lax.axis_index("tensor")
    x, y, c = f // 8, lax.rem(f // 2, 4), lax.rem(f, 2)
    q_me = 4 * x + y

    def mod(i):
        return lax.rem(i + 8, 4)

    def dev(xx, yy, cc, zz):
        return (mod(xx) * 8 + mod(yy) * 2 + cc, mod(zz))

    sib = dev(x, y, 1 - c, z)
    n_used = [0]

    def take(n):
        at = n_used[0]
        n_used[0] += n
        assert n_used[0] <= N_SEM
        return at

    def send(src, dst, to, i):
        return pltpu.make_async_remote_copy(
            src_ref=src, dst_ref=dst, send_sem=ss.at[i], recv_sem=rs.at[i],
            device_id=to, device_id_type=MESH,
        )

    pending = []

    def start(src, dst, to, i):
        copy = send(src, dst, to, i)
        copy.start()
        pending.append(copy)

    def arrived(dst, i):
        send(dst, dst, sib, i).wait_recv()

    def sent():
        for copy in pending:
            copy.wait_send()
        pending.clear()

    bar = pltpu.get_barrier_semaphore()
    peers = [sib]
    for d in (1, 2, 3):
        peers += [dev(x + d, y, c, z), dev(x, y + d, c, z), dev(x, y, c, z + d)]
    for peer in peers:
        pl.semaphore_signal(bar, inc=1, device_id=peer, device_id_type=MESH)
    loads = []
    for h in range(2):
        half = (1 - c) if h == 0 else c
        at = pl.ds(pl.multiple_of(half * HALF, 128), HALF)
        loads.append(pltpu.make_async_copy(m_hbm.at[:, at], m_v.at[h], ls.at[2 * h]))
        loads.append(pltpu.make_async_copy(g_hbm.at[:, at], g_v.at[h], ls.at[2 * h + 1]))
    for load in loads:
        load.start()
    pl.semaphore_wait(bar, len(peers))

    def ab(s):
        return (x, y) if s == 0 else (y, x)

    def dev_ab(s, a, b):
        return dev(a, b, c, z) if s == 0 else dev(b, a, c, z)

    class Gather:
        def __init__(self, piece, half, own, after=None):
            self.piece, self.half, self.own = piece, half, own
            self.small = [take(3), take(3)]
            self.big = [take(8), take(8)]
            self.forward = [take(8), take(8)]

        def spread(self, s, k, src):
            a, b = ab(s)
            here = self.piece(s, a, mod(b + k))
            start(src, here, dev_ab(s, a + 1, b), self.big[s] + k)
            start(src, here, dev_ab(s, a - 1, b), self.big[s] + 4 + k)

        def begin(self):
            for s in range(2):
                a, b = ab(s)
                for d in (1, 3, 2):
                    start(self.own(s), self.piece(s, a, b), dev_ab(s, a, b + d), self.small[s] + d - 1)
                self.spread(s, 0, self.own(s))

        def middle(self, d):
            for s in range(2):
                a, b = ab(s)
                piece = self.piece(s, a, mod(b - d))
                arrived(piece, self.small[s] + d - 1)
                self.spread(s, 4 - d, piece)

        def relay(self, k):
            for s in range(2):
                a, b = ab(s)
                bb = mod(b + k)
                arrived(self.piece(s, mod(a - 1), bb), self.big[s] + k)
                plus = self.half(s, mod(a - 1), bb, 0)
                start(plus, plus, dev_ab(s, a + 1, b), self.forward[s] + k)
                arrived(self.piece(s, mod(a + 1), bb), self.big[s] + 4 + k)
                minus = self.half(s, mod(a + 1), bb, 1)
                start(minus, minus, dev_ab(s, a - 1, b), self.forward[s] + 4 + k)

        def finish(self, k):
            for s in range(2):
                a, b = ab(s)
                bb = mod(b + k)
                arrived(self.half(s, mod(a + 2), bb, 0), self.forward[s] + k)
                arrived(self.half(s, mod(a + 2), bb, 1), self.forward[s] + 4 + k)

    i_v = take(2)
    for s in range(2):
        theirs = pl.ds(pl.multiple_of((1 - c) * HALF + s * STREAM, 128), STREAM)
        start(v_in.at[:, theirs], vb.at[s, q_me, pl.ds(8 * c, 8)], sib, i_v + s)
    for s in range(2):
        mine = pl.ds(pl.multiple_of(c * HALF + s * STREAM, 128), STREAM)
        vb[s, q_me, pl.ds(pl.multiple_of(8 * c, 8), 8), :] = v_in[:, mine]
    for s in range(2):
        arrived(vb.at[s, q_me, pl.ds(8 * (1 - c), 8)], i_v + s)

    def v_piece(s, a, b):
        return vb.at[s, 4 * a + b] if s == 0 else vb.at[s, 4 * b + a]

    def v_half(s, a, b, h):
        return v_piece(s, a, b).at[pl.ds(8 * h, 8)]

    gather_v = Gather(v_piece, v_half, lambda s: v_piece(s, *ab(s)))
    gather_v.begin()

    i_b = take(N_CHUNK)
    loads[0].wait()
    loads[1].wait()

    def b_send(j):
        return send(bts.at[j], btr.at[j], sib, i_b + j)

    def other_chunk(j, carry):
        at = pl.ds(pl.multiple_of(j * CHUNK, CHUNK), CHUNK)
        bts[j] = (m_v[0, :, at] + g_v[0, :, at].astype(F32)).T
        b_send(j).start()
        return carry

    def own_chunk(j, carry):
        at = pl.ds(pl.multiple_of(j * CHUNK, CHUNK), CHUNK)
        high, low = split((m_v[1, :, at] + g_v[1, :, at].astype(F32)).T)
        bh[at, 0:ROWS] = high
        bl[at, 0:ROWS] = low
        return carry

    def sibling_chunk(j, carry):
        b_send(j).wait()
        at = pl.ds(pl.multiple_of(j * CHUNK, CHUNK), CHUNK)
        high, low = split(btr[j])
        bh[at, ROWS:] = high
        bl[at, ROWS:] = low
        return carry

    lax.fori_loop(0, N_CHUNK, other_chunk, 0)
    gather_v.middle(1)
    gather_v.middle(3)
    gather_v.middle(2)
    loads[2].wait()
    loads[3].wait()
    lax.fori_loop(0, N_CHUNK, own_chunk, 0)
    gather_v.relay(0)
    lax.fori_loop(0, N_CHUNK, sibling_chunk, 0)
    for k in (3, 1, 2):
        gather_v.relay(k)
    for k in (0, 3, 1, 2):
        gather_v.finish(k)

    for s in range(2):
        span = slice(s * STREAM, (s + 1) * STREAM)

        def project(g, carry):
            rows = vb[s, pl.ds(4 * g, 4)].reshape(64, STREAM)
            high, low = split(rows)
            part = dot(high, bh[span, :]) + dot(high, bl[span, :]) + dot(low, bh[span, :])
            at = pl.ds(pl.multiple_of(64 * g, 64), 64)
            if s == 0:
                pt[at, :] = part
            else:
                pt[at, :] = pt[at, :] + part
            return carry

        lax.fori_loop(0, 4, project, 0)
    sent()
    i_p = take(1)
    start(pt.at[:, ROWS:], ptr, sib, i_p)
    arrived(ptr, i_p)
    zr[0] = pt[:, 0:ROWS] + ptr[...]
    near = z + 1 - 2 * lax.rem(z, 2)
    far = 3 - z
    i_z = take(4)
    tops = (pl.ds(0, 128), pl.ds(128, 128))
    for step in range(2):
        for h in range(2):
            to = near if h == step else far
            start(zr.at[2 * step, tops[h]], zr.at[2 * step + 1, tops[h]], dev(x, y, c, to), i_z + 2 * step + h)
        for h in range(2):
            arrived(zr.at[2 * step + 1, tops[h]], i_z + 2 * step + h)
            zr[2 * step + 2, tops[h], :] = zr[2 * step, tops[h], :] + zr[2 * step + 1, tops[h], :]
    p_own = zr.at[4]
    i_s = take(1)
    start(p_own, pts, sib, i_s)
    high, low = split(p_own[...].T)
    ph[0:ROWS, :] = high
    plo[0:ROWS, :] = low
    arrived(pts, i_s)
    high, low = split(pts[...].T)
    ph[ROWS:, :] = high
    plo[ROWS:, :] = low

    def exchange(slots, at, where, i):
        for d in (1, 2, 3):
            start(slots.at[at], slots.at[at], where(at + d), i + d - 1)

    def exchanged(slots, at, i):
        for d in (1, 2, 3):
            arrived(slots.at[mod(at - d)], i + d - 1)
        return slots[0] + slots[1] + slots[2] + slots[3]

    share = pl.ds(pl.multiple_of(32 * (2 * z + c), 32), 32)
    gx[x] = dot_nt(zr[4, share, :], p_own[...], HIGHEST) + dot_nt(pts[share, :], pts[...], HIGHEST)
    i_gx, i_gy, i_gz, i_gc = take(3), take(3), take(3), take(1)
    exchange(gx, x, lambda to: dev(to, y, c, z), i_gx)

    def right_part(s, a):
        row = pl.multiple_of(s * STREAM + a * 4 * PIECE, 16)
        at = pl.ds(row, 4 * PIECE)
        part = dot(bh[at, :], ph[...]) + dot(bh[at, :], plo[...]) + dot(bl[at, :], ph[...])
        wt[pl.ds(16 * s + 4 * a, 4)] = part.reshape(4, PIECE, RANK)

    i_r1, i_r2, i_r3 = take(4), take(4), take(6)
    low_cut, high_cut = pl.ds(0, CUT), pl.ds(CUT, PIECE - CUT)

    def group(s, a):
        return pl.ds(16 * s + 4 * mod(a), 4)

    for s in range(2):
        a, b = ab(s)
        right_part(s, mod(a + 2))
        start(wt.at[group(s, a + 2), low_cut], r1p.at[s], dev_ab(s, a + 1, b), i_r1 + 2 * s)
        start(wt.at[group(s, a + 2), high_cut], r1m.at[s], dev_ab(s, a - 1, b), i_r1 + 2 * s + 1)
    for s in range(2):
        a, b = ab(s)
        right_part(s, mod(a + 1))
        right_part(s, mod(a - 1))
    gy[y] = exchanged(gx, x, i_gx)
    exchange(gy, y, lambda to: dev(x, to, c, z), i_gy)
    for s in range(2):
        a, b = ab(s)
        right_part(s, a)
    for s in range(2):
        a, b = ab(s)
        up, down = group(s, a + 1), group(s, a - 1)
        arrived(r1p.at[s], i_r1 + 2 * s)
        wt[up, 0:CUT, :] = wt[up, 0:CUT, :] + r1p[s]
        start(wt.at[up], r2.at[s, 0], dev_ab(s, a + 1, b), i_r2 + 2 * s)
        arrived(r1m.at[s], i_r1 + 2 * s + 1)
        wt[down, CUT:, :] = wt[down, CUT:, :] + r1m[s]
        start(wt.at[down], r2.at[s, 1], dev_ab(s, a - 1, b), i_r2 + 2 * s + 1)
    gg[z, c] = exchanged(gy, y, i_gy)
    for d in (1, 2, 3):
        start(gg.at[z, c], gg.at[z, c], dev(x, y, c, z + d), i_gz + d - 1)
    for d in (1, 2, 3):
        arrived(gg.at[mod(z - d), c], i_gz + d - 1)
    start(gg.at[:, c], gg.at[:, c], sib, i_gc)
    arrived(gg.at[:, 1 - c], i_gc)
    work[:, 0:RANK] = gg[...].reshape(RANK, RANK)
    eye = lax.broadcasted_iota(jnp.int32, (RANK, RANK), 0) == lax.broadcasted_iota(
        jnp.int32, (RANK, RANK), 1
    )
    work[:, RANK:] = eye.astype(F32)

    def panels(base, low, high):
        def one(p, carry):
            factor_panel(work, base, p)
            return carry

        lax.fori_loop(low, high, one, 0)

    panels(0, 0, 8)

    def own_idx(s):
        a, b = ab(s)
        return 16 * s + 4 * a + b

    for s in range(2):
        a, b = ab(s)
        here = group(s, a)
        for k in range(2):
            arrived(r2.at[s, k], i_r2 + 2 * s + k)
        wt[here] = wt[here] + r2[s, 0] + r2[s, 1]
        for d in (1, 3, 2):
            start(wt.at[16 * s + 4 * a + mod(b + d)], r3.at[s, d - 1], dev_ab(s, a, b + d), i_r3 + 3 * s + d - 1)
    panels(0, 8, 12)
    keeps = []
    for s in range(2):
        for d in (1, 3, 2):
            arrived(r3.at[s, d - 1], i_r3 + 3 * s + d - 1)
        wown[s] = wt[own_idx(s)] + r3[s, 0] + r3[s, 1] + r3[s, 2]
        keep = pltpu.make_async_copy(wown.at[s], wt_out.at[32 * c + own_idx(s)], ls.at[4 + s])
        keep.start()
        keeps.append(keep)

    def w_piece(s, a, b):
        return wt_out.at[32 * c + 16 * s + 4 * a + b]

    def w_half(s, a, b, h):
        return w_piece(s, a, b).at[low_cut if h == 0 else high_cut]

    i_w = take(8)

    def hand_over(n, a_of):
        for s in range(2):
            a = a_of(ab(s)[0])
            at = wt_out.at[pl.ds(32 * c + 16 * s + 4 * a, 4)]
            start(at, at, sib, i_w + 2 * n + s)

    gather_w = Gather(w_piece, w_half, lambda s: wown.at[s])
    gather_w.begin()
    panels(0, 12, 16)
    work[128:, :] = work[128:, :] - dot_tn(work[0:128, 128:256], work[0:128, :], HIGHEST)
    gather_w.middle(1)
    gather_w.middle(3)
    gather_w.middle(2)
    for keep in keeps:
        keep.wait()
    hand_over(0, lambda a: a)
    panels(128, 0, 6)
    gather_w.relay(0)
    panels(128, 6, 12)
    gather_w.relay(3)
    panels(128, 12, 16)
    gather_w.relay(1)

    low_inv = work.at[:, pl.ds(RANK, RANK)]
    total = jnp.zeros((1, RANK), F32)
    for s in range(2):
        right = dot_nt(wown[s], low_inv[...], HIGHEST)
        total = total + jnp.sum(right * right, axis=0, keepdims=True)
    i_qx, i_qy, i_qz, i_qc = take(3), take(3), take(3), take(1)
    sx[x] = jnp.broadcast_to(total, (8, RANK))
    exchange(sx, x, lambda to: dev(to, y, c, z), i_qx)
    gather_w.relay(2)
    hand_over(1, lambda a: mod(a - 1))
    hand_over(2, lambda a: mod(a + 1))
    q_s[...] = dot_nt(jnp.transpose(p_own[...]), low_inv[...], HIGHEST)
    lhs_out[ROWS:, :] = -0.05 * dot(q_s[...], low_inv[...], HIGHEST)
    sy[y] = exchanged(sx, x, i_qx)
    exchange(sy, y, lambda to: dev(x, to, c, z), i_qy)
    sz[z] = exchanged(sy, y, i_qy)
    exchange(sz, z, lambda to: dev(x, y, c, to), i_qz)
    sc[c] = exchanged(sz, z, i_qz)
    start(sc.at[c], sc.at[c], sib, i_qc)
    arrived(sc.at[1 - c], i_qc)
    norm = 1.0 / (jnp.sqrt((sc[0] + sc[1])[0:1, :]) + 1e-06)
    unit_scale = (M_ROWS * N_COLS / RANK) ** 0.5
    lhs_out[0:ROWS, :] = dot(q_s[...] * (unit_scale * norm), low_inv[...], HIGHEST)
    pick = lax.broadcasted_iota(jnp.int32, (16, RANK), 1) == (
        8 * f + lax.broadcasted_iota(jnp.int32, (16, RANK), 0)
    )
    m8_out[...] = dot(jnp.where(pick, norm, 0.0), low_inv[...], HIGHEST)
    for k in (0, 3, 1, 2):
        gather_w.finish(k)
    hand_over(3, lambda a: mod(a + 2))
    for n, step in enumerate((0, -1, 1, 2)):
        for s in range(2):
            a = mod(ab(s)[0] + step)
            arrived(wt_out.at[pl.ds(32 * (1 - c) + 16 * s + 4 * a, 4)], i_w + 2 * n + s)
    sent()


def reduce_right(momentum, gradient, right_prev):
    vmem = pltpu.VMEM
    any_space = pl.BlockSpec(memory_space=pl.ANY)
    in_vmem = pl.BlockSpec(memory_space=pltpu.VMEM)
    return pl.pallas_call(
        kernel,
        out_shape=(
            jax.ShapeDtypeStruct((64, PIECE, RANK), F32),
            jax.ShapeDtypeStruct((2 * ROWS, RANK), F32),
            jax.ShapeDtypeStruct((16, RANK), F32),
        ),
        in_specs=[any_space, any_space, in_vmem],
        out_specs=(any_space, in_vmem, in_vmem),
        scratch_shapes=[
            vmem((2, ROWS, HALF), F32),
            vmem((2, ROWS, HALF), BF16),
            vmem((N_CHUNK, CHUNK, ROWS), F32),
            vmem((N_CHUNK, CHUNK, ROWS), F32),
            vmem((HALF, 2 * ROWS), BF16),
            vmem((HALF, 2 * ROWS), BF16),
            vmem((2, 16, 16, STREAM), F32),
            vmem((RANK, 2 * ROWS), F32),
            vmem((RANK, ROWS), F32),
            vmem((5, RANK, ROWS), F32),
            vmem((RANK, ROWS), F32),
            vmem((2 * ROWS, RANK), BF16),
            vmem((2 * ROWS, RANK), BF16),
            vmem((4, 32, RANK), F32),
            vmem((4, 32, RANK), F32),
            vmem((4, 2, 32, RANK), F32),
            vmem((32, PIECE, RANK), F32),
            vmem((2, 4, CUT, RANK), F32),
            vmem((2, 4, PIECE - CUT, RANK), F32),
            vmem((2, 2, 4, PIECE, RANK), F32),
            vmem((2, 3, PIECE, RANK), F32),
            vmem((2, PIECE, RANK), F32),
            vmem((RANK, 2 * RANK), F32),
            vmem((4, 8, RANK), F32),
            vmem((4, 8, RANK), F32),
            vmem((4, 8, RANK), F32),
            vmem((2, 8, RANK), F32),
            vmem((ROWS, RANK), F32),
            pltpu.SemaphoreType.DMA((N_SEM,)),
            pltpu.SemaphoreType.DMA((N_SEM,)),
            pltpu.SemaphoreType.DMA((6,)),
        ],
        compiler_params=pltpu.CompilerParams(
            collective_id=0, has_side_effects=True, vmem_limit_bytes=56 * 2**20
        ),
        name="reduce_right",
    )(momentum, gradient, right_prev)


def finish_kernel(m_ref, g_ref, wt_ref, lhs_ref, m8_ref, new_ref, right_ref, update_ref):
    high, low = split(wt_ref[...])
    lhs_high, lhs_low = split(lhs_ref[0:ROWS, :])
    feed = lhs_ref[ROWS:, :].astype(BF16)
    new_ref[...] = m_ref[...] + g_ref[...].astype(F32) + dot_nt(feed, high)
    update = dot_nt(lhs_high, high) + dot_nt(lhs_high, low) + dot_nt(lhs_low, high)
    update_ref[...] = update.astype(BF16)
    m8_high, m8_low = split(m8_ref[...])
    right = dot_nt(m8_high, high) + dot_nt(m8_high, low) + dot_nt(m8_low, high)
    right_ref[...] = right[0:8, :]


def finish(momentum, gradient, wt, lhs, m8):
    wide = 512
    return pl.pallas_call(
        finish_kernel,
        grid=(COLS // wide,),
        out_shape=(
            jax.ShapeDtypeStruct((ROWS, COLS), F32),
            jax.ShapeDtypeStruct((8, COLS), F32),
            jax.ShapeDtypeStruct((ROWS, COLS), BF16),
        ),
        in_specs=[
            pl.BlockSpec((ROWS, wide), lambda j: (0, j)),
            pl.BlockSpec((ROWS, wide), lambda j: (0, j)),
            pl.BlockSpec((wide, RANK), lambda j: (j, 0)),
            pl.BlockSpec((2 * ROWS, RANK), lambda j: (0, 0)),
            pl.BlockSpec((16, RANK), lambda j: (0, 0)),
        ],
        out_specs=(
            pl.BlockSpec((ROWS, wide), lambda j: (0, j)),
            pl.BlockSpec((8, wide), lambda j: (0, j)),
            pl.BlockSpec((ROWS, wide), lambda j: (0, j)),
        ),
        compiler_params=pltpu.CompilerParams(vmem_limit_bytes=32 * 2**20),
        name="finish",
    )(momentum, gradient, wt, lhs, m8)


def on_device(momentum, gradient, right_prev):
    wt, lhs, m8 = reduce_right(momentum, gradient, right_prev)
    return finish(momentum, gradient, wt.reshape(COLS, RANK), lhs, m8)


def solution(mesh):
    spec = P("fsdp", "tensor")
    return jax.shard_map(
        on_device, mesh=mesh, in_specs=(spec,) * 3, out_specs=(spec,) * 3, check_vma=False
    )
```

```python
import jax
import jax.numpy as jnp
from jax import lax
from jax.experimental import pallas as pl
from jax.experimental.pallas import tpu as pltpu
from jax.sharding import PartitionSpec as P

M_ROWS = 8192
N_COLS = 26624
RANK = 256
F32 = jnp.float32
BF16 = jnp.bfloat16
MESH = pl.DeviceIdType.MESH
HIGHEST = lax.Precision.HIGHEST

ROWS = 256
COLS = 6656
HALF = COLS // 2
STREAM = HALF // 2
PIECE = STREAM // 16
V_SUB = ((0, 896), (896, STREAM - 896))
W_SUB = ((0, 56), (56, 48))
W_HALF = (((0, 32), (32, 24)), ((56, 24), (80, 24)))
MAIN_MIB = 42
FINISH_MIB = 22
WIDE = 1664
BLOCK = 16
CHUNK = 256
N_CHUNK = HALF // CHUNK
N_SEM = 288

def split(a):
    high = a.astype(BF16)
    return high, (a - high.astype(F32)).astype(BF16)

def dot(a, b, precision=None):
    return jnp.dot(a, b, precision=precision, preferred_element_type=F32)

def dot_nt(a, b, precision=None):
    return lax.dot_general(
        a, b, (((1,), (1,)), ((), ())), precision=precision, preferred_element_type=F32
    )

def dot_tn(a, b, precision=None):
    return lax.dot_general(
        a, b, (((0,), (0,)), ((), ())), precision=precision, preferred_element_type=F32
    )

def row_of(v, i):
    return jnp.broadcast_to(v[i : i + 1, :], v.shape)

def thirds(a):
    one = a.astype(BF16).astype(F32)
    rest = a - one
    two = rest.astype(BF16).astype(F32)
    return one, two, rest - two

def outer(left, right):
    l1, l2, l3 = thirds(left)
    r1, r2, r3 = thirds(right)
    a = jnp.concatenate([l1, l1, l2, l1, l2, l3], axis=0).astype(BF16)
    b = jnp.concatenate([r1, r2, r1, r3, r2, r1], axis=0).astype(BF16)
    return dot_tn(a, b)

def factor_panel(work, base, panel):
    first = base + BLOCK * panel
    sub = lax.broadcasted_iota(jnp.int32, (BLOCK, 128), 0)
    lane = lax.broadcasted_iota(jnp.int32, (BLOCK, 128), 1)
    rows = pl.ds(pl.multiple_of(first, BLOCK), BLOCK)
    parts = [work[rows, 128 * t : 128 * t + 128] for t in range(4)]
    here = pltpu.roll(parts[base // 128], lax.rem(128 - BLOCK * panel, 128), 1)
    cols = [jnp.broadcast_to(here[:, i : i + 1], (BLOCK, 128)) for i in range(BLOCK)]
    for i in range(BLOCK):
        inv = lax.rsqrt(row_of(cols[i], i))
        coef = jnp.where(sub > i, cols[i] * inv, 0.0)
        for t in range(4):
            scaled = row_of(parts[t], i) * inv
            parts[t] = jnp.where(sub == i, scaled, parts[t] - coef * scaled)
        for j in range(i + 1, BLOCK):
            cols[j] = cols[j] - coef * (row_of(cols[j], i) * inv)
    for t in range(4):
        work[rows, 128 * t : 128 * t + 128] = parts[t]
    left = jnp.where(lane > BLOCK * panel + BLOCK - 1, parts[base // 128], 0.0)
    whole = jnp.concatenate(parts, axis=1)
    work[base : base + 128, :] = work[base : base + 128, :] - outer(left, whole)

def kernel(
    m_hbm, g_hbm, v_hbm, wt_out, lhs_out,
    m_v, g_v, v_in, bts, btr, bh, bl, vb, pt, pst, ptr, zr, pts, ph, plo,
    gx, gy, gg, wt, r1, r2, r3, wown, work, sx, sy, sz, sc, q_s,
    ss, rs, ls,
):
    f = lax.axis_index("fsdp")
    z = lax.axis_index("tensor")
    x, y, c = f // 8, lax.rem(f // 2, 4), lax.rem(f, 2)

    def mod(i):
        return lax.rem(i + 8, 4)

    def dev(xx, yy, cc, zz):
        return (mod(xx) * 8 + mod(yy) * 2 + cc, mod(zz))

    sib = dev(x, y, 1 - c, z)
    n_used = [0]

    def take(n):
        at = n_used[0]
        n_used[0] += n
        assert n_used[0] <= N_SEM
        return at

    def send(src, dst, to, i):
        return pltpu.make_async_remote_copy(
            src_ref=src, dst_ref=dst, send_sem=ss.at[i], recv_sem=rs.at[i],
            device_id=to, device_id_type=MESH,
        )

    pending = []

    def start(src, dst, to, i):
        copy = send(src, dst, to, i)
        copy.start()
        pending.append(copy)

    def arrived(dst, i):
        send(dst, dst, sib, i).wait_recv()

    def sent():
        for copy in pending:
            copy.wait_send()
        pending.clear()

    bar = pltpu.get_barrier_semaphore()
    peers = [sib]
    for d in (1, 2, 3):
        peers += [dev(x + d, y, c, z), dev(x, y + d, c, z), dev(x, y, c, z + d)]
    for peer in peers:
        pl.semaphore_signal(bar, inc=1, device_id=peer, device_id_type=MESH)
    v_load = pltpu.make_async_copy(v_hbm, v_in, ls.at[6])
    v_load.start()
    loads = []
    for h in range(2):
        half = (1 - c) if h == 0 else c
        at = pl.ds(pl.multiple_of(half * HALF, 128), HALF)
        loads.append(pltpu.make_async_copy(m_hbm.at[:, at], m_v.at[h], ls.at[2 * h]))
        loads.append(pltpu.make_async_copy(g_hbm.at[:, at], g_v.at[h], ls.at[2 * h + 1]))
    for load in loads:
        load.start()
    v_load.wait()
    pl.semaphore_wait(bar, len(peers))

    def ab(s):
        return (x, y) if s == 0 else (y, x)

    def dev_ab(s, a, b):
        return dev(a, b, c, z) if s == 0 else dev(b, a, c, z)

    class Gather:
        def __init__(self, piece, half, own):
            self.piece, self.half, self.own = piece, half, own
            self.small, self.big, self.forward = take(12), take(32), take(32)

        def i_small(self, s, u, d):
            return self.small + 6 * s + 3 * u + d - 1

        def i_big(self, s, u, way, k):
            return self.big + 16 * s + 8 * u + 4 * way + k

        def i_forward(self, s, u, way, k):
            return self.forward + 16 * s + 8 * u + 4 * way + k

        def begin(self, u):
            for s in range(2):
                a, b = ab(s)
                for d in (1, 3, 2):
                    start(self.own(s, u), self.piece(s, a, b, u), dev_ab(s, a, b + d), self.i_small(s, u, d))

        def spread(self, s, u, k, src):
            a, b = ab(s)
            here = self.piece(s, a, mod(b + k), u)
            start(src, here, dev_ab(s, a + 1, b), self.i_big(s, u, 0, k))
            start(src, here, dev_ab(s, a - 1, b), self.i_big(s, u, 1, k))

        def middle(self, u, d):
            for s in range(2):
                a, b = ab(s)
                piece = self.piece(s, a, mod(b - d), u)
                arrived(piece, self.i_small(s, u, d))
                if d == 1:
                    self.spread(s, u, 0, self.own(s, u))
                self.spread(s, u, 4 - d, piece)

        def relay(self, u, k):
            for s in range(2):
                a, b = ab(s)
                bb = mod(b + k)
                for way, step in ((0, 1), (1, -1)):
                    arrived(self.piece(s, mod(a - step), bb, u), self.i_big(s, u, way, k))
                    part = self.half(s, mod(a - step), bb, u, way)
                    start(part, part, dev_ab(s, a + step, b), self.i_forward(s, u, way, k))

        def finish(self, u, k):
            for s in range(2):
                a, b = ab(s)
                for way in range(2):
                    arrived(self.half(s, mod(a + 2), mod(b + k), u, way), self.i_forward(s, u, way, k))

    i_v = take(2)
    for s in range(2):
        theirs = pl.ds(pl.multiple_of((1 - c) * HALF + s * STREAM, 128), STREAM)
        start(v_in.at[:, theirs], vb.at[s, x, y, pl.ds(8 * c, 8)], sib, i_v + s)
    for s in range(2):
        mine = pl.ds(pl.multiple_of(c * HALF + s * STREAM, 128), STREAM)
        vb[s, x, y, pl.ds(pl.multiple_of(8 * c, 8), 8), :] = v_in[:, mine]
    for s in range(2):
        arrived(vb.at[s, x, y, pl.ds(8 * (1 - c), 8)], i_v + s)

    def v_piece(s, a, b, u):
        at = (s, a, b) if s == 0 else (s, b, a)
        return vb.at[(*at, slice(None), pl.ds(*V_SUB[u]))]

    def v_half(s, a, b, u, h):
        return v_piece(s, a, b, u).at[pl.ds(8 * h, 8)]

    gather_v = Gather(v_piece, v_half, lambda s, u: v_piece(s, *ab(s), u))
    gather_v.begin(0)
    gather_v.begin(1)

    i_b = take(N_CHUNK)
    loads[0].wait()
    loads[1].wait()

    def b_send(j):
        return send(bts.at[j], btr.at[j], sib, i_b + j)

    def other_chunk(j, carry):
        at = pl.ds(pl.multiple_of(j * CHUNK, CHUNK), CHUNK)
        bts[j] = (m_v[0, :, at] + g_v[0, :, at].astype(F32)).T
        b_send(j).start()
        return carry

    def own_chunk(j, carry):
        at = pl.ds(pl.multiple_of(j * CHUNK, CHUNK), CHUNK)
        high, low = split((m_v[1, :, at] + g_v[1, :, at].astype(F32)).T)
        bh[at, 0:ROWS] = high
        bl[at, 0:ROWS] = low
        return carry

    def sibling_chunk(j, carry):
        b_send(j).wait()
        at = pl.ds(pl.multiple_of(j * CHUNK, CHUNK), CHUNK)
        high, low = split(btr[j])
        bh[at, ROWS:] = high
        bl[at, ROWS:] = low
        return carry

    def project(a_of):
        for s in range(2):
            span = slice(s * STREAM, (s + 1) * STREAM)
            a = a_of(ab(s)[0])
            rows = (vb[s, a] if s == 0 else vb[s, :, a]).reshape(64, STREAM)
            high, low = split(rows)
            both = dot(jnp.concatenate([high, low], axis=0), bh[span, :])
            part = (both[0:64] + both[64:] + dot(high, bl[span, :])).reshape(4, 16, 2 * ROWS)
            if s == 0:
                pt[s, a] = part
            else:
                pt[s, :, a] = part

    lax.fori_loop(0, N_CHUNK, other_chunk, 0)
    for d in (1, 3, 2):
        for u in range(2):
            gather_v.middle(u, d)
    loads[2].wait()
    loads[3].wait()
    lax.fori_loop(0, N_CHUNK, own_chunk, 0)
    for u in range(2):
        gather_v.relay(u, 0)
    lax.fori_loop(0, N_CHUNK, sibling_chunk, 0)
    for k in (3, 1):
        for u in range(2):
            gather_v.relay(u, k)
    project(lambda a: a)
    for u in range(2):
        gather_v.relay(u, 2)
    project(lambda a: mod(a - 1))
    project(lambda a: mod(a + 1))
    for k in (0, 3, 1, 2):
        for u in range(2):
            gather_v.finish(u, k)

    project(lambda a: mod(a + 2))
    sent()

    i_p = take(1)
    pst[...] = (pt[0, :, :, :, ROWS:] + pt[1, :, :, :, ROWS:]).reshape(RANK, ROWS)
    start(pst, ptr, sib, i_p)
    mine = (pt[0, :, :, :, 0:ROWS] + pt[1, :, :, :, 0:ROWS]).reshape(RANK, ROWS)
    arrived(ptr, i_p)
    zr[0] = mine + ptr[...]
    near = z + 1 - 2 * lax.rem(z, 2)
    far = 3 - z
    i_z = take(4)
    tops = (pl.ds(0, 128), pl.ds(128, 128))
    for step in range(2):
        for h in range(2):
            to = near if h == step else far
            start(zr.at[2 * step, tops[h]], zr.at[2 * step + 1, tops[h]], dev(x, y, c, to), i_z + 2 * step + h)
        for h in range(2):
            arrived(zr.at[2 * step + 1, tops[h]], i_z + 2 * step + h)
            zr[2 * step + 2, tops[h], :] = zr[2 * step, tops[h], :] + zr[2 * step + 1, tops[h], :]
    p_own = zr.at[4]
    i_s = take(1)
    start(p_own, pts, sib, i_s)
    high, low = split(p_own[...].T)
    ph[0:ROWS, :] = high
    plo[0:ROWS, :] = low
    arrived(pts, i_s)
    high, low = split(pts[...].T)
    ph[ROWS:, :] = high
    plo[ROWS:, :] = low

    def exchange(slots, at, where, i):
        for d in (1, 2, 3):
            start(slots.at[at], slots.at[at], where(at + d), i + d - 1)

    def exchanged(slots, at, i):
        for d in (1, 2, 3):
            arrived(slots.at[mod(at - d)], i + d - 1)
        return slots[0] + slots[1] + slots[2] + slots[3]

    share = pl.ds(pl.multiple_of(32 * (2 * z + c), 32), 32)
    gx[x] = dot_nt(zr[4, share, :], p_own[...], HIGHEST) + dot_nt(pts[share, :], pts[...], HIGHEST)
    i_gx, i_gy, i_gz, i_gc = take(3), take(3), take(3), take(1)
    exchange(gx, x, lambda to: dev(to, y, c, z), i_gx)

    def right_part(s, a):
        row = pl.multiple_of(s * STREAM + a * 4 * PIECE, 16)
        at = pl.ds(row, 4 * PIECE)
        part = dot(bh[at, :], ph[...]) + dot(bh[at, :], plo[...]) + dot(bl[at, :], ph[...])
        wt[pl.ds(16 * s + 4 * a, 4)] = part.reshape(4, PIECE, RANK)

    i_r1, i_r2, i_r3 = take(8), take(8), take(12)

    def group(s, a):
        return pl.ds(16 * s + 4 * mod(a), 4)

    def first_sends(s):
        a, b = ab(s)
        for u in range(2):
            for way, step in ((0, 1), (1, -1)):
                part = pl.ds(*W_HALF[u][way])
                start(wt.at[group(s, a + 2), part], r1.at[s, :, part], dev_ab(s, a + step, b), i_r1 + 4 * s + 2 * u + way)

    def second_sends(u):
        sub = pl.ds(*W_SUB[u])
        for s in range(2):
            a, b = ab(s)
            for way, step in ((0, 1), (1, -1)):
                part = pl.ds(*W_HALF[u][way])
                arrived(r1.at[s, :, part], i_r1 + 4 * s + 2 * u + way)
                at = group(s, a + step)
                wt[at, part, :] = wt[at, part, :] + r1[s, :, part, :]
                start(wt.at[at, sub], r2.at[s, way, :, sub], dev_ab(s, a + step, b), i_r2 + 4 * s + 2 * u + way)

    def third_sends(u):
        sub = pl.ds(*W_SUB[u])
        for s in range(2):
            a, b = ab(s)
            for way in range(2):
                arrived(r2.at[s, way, :, sub], i_r2 + 4 * s + 2 * u + way)
            here = group(s, a)
            wt[here, sub, :] = wt[here, sub, :] + r2[s, 0, :, sub, :] + r2[s, 1, :, sub, :]
            for d in (1, 3, 2):
                start(wt.at[16 * s + 4 * a + mod(b + d), sub], r3.at[s, d - 1, sub], dev_ab(s, a, b + d), i_r3 + 6 * s + 3 * u + d - 1)

    keeps = []

    def own_sums(u):
        sub = pl.ds(*W_SUB[u])
        for s in range(2):
            a, b = ab(s)
            for d in (1, 3, 2):
                arrived(r3.at[s, d - 1, sub], i_r3 + 6 * s + 3 * u + d - 1)
            own = 16 * s + 4 * a + b
            wown[s, sub, :] = wt[own, sub, :] + r3[s, 0, sub, :] + r3[s, 1, sub, :] + r3[s, 2, sub, :]
            keep = pltpu.make_async_copy(wown.at[s, sub], wt_out.at[32 * c + own, sub], ls.at[7 + 2 * s + u])
            keep.start()
            keeps.append(keep)

    def w_piece(s, a, b, u):
        return wt_out.at[32 * c + 16 * s + 4 * a + b, pl.ds(*W_SUB[u])]

    def w_half(s, a, b, u, h):
        return wt_out.at[32 * c + 16 * s + 4 * a + b, pl.ds(*W_HALF[u][h])]

    gather_w = Gather(w_piece, w_half, lambda s, u: wown.at[s, pl.ds(*W_SUB[u])])
    i_w = take(8)

    def hand_over(n, step):
        for s in range(2):
            at = wt_out.at[pl.ds(32 * c + 16 * s + 4 * mod(ab(s)[0] + step), 4)]
            start(at, at, sib, i_w + 2 * n + s)

    def panels(low, high):
        def one(base):
            def body(p, carry):
                factor_panel(work, base, p)
                return carry

            return body

        per = 128 // BLOCK
        if low < per:
            lax.fori_loop(low, min(high, per), one(0), 0)
        if low < per <= high:
            work[128:, :] = work[128:, :] - dot_tn(work[0:128, 128:256], work[0:128, :], HIGHEST)
        if high > per:
            lax.fori_loop(max(low, per) - per, high - per, one(128), 0)

    for s in range(2):
        right_part(s, mod(ab(s)[0] + 2))
        first_sends(s)
    for s in range(2):
        right_part(s, mod(ab(s)[0] + 1))
        right_part(s, mod(ab(s)[0] - 1))
    gy[y] = exchanged(gx, x, i_gx)
    exchange(gy, y, lambda to: dev(x, to, c, z), i_gy)
    for s in range(2):
        right_part(s, ab(s)[0])
    second_sends(0)
    gg[z, c] = exchanged(gy, y, i_gy)
    for d in (1, 2, 3):
        start(gg.at[z, c], gg.at[z, c], dev(x, y, c, z + d), i_gz + d - 1)
    second_sends(1)
    for d in (1, 2, 3):
        arrived(gg.at[mod(z - d), c], i_gz + d - 1)
    start(gg.at[:, c], gg.at[:, c], sib, i_gc)
    eye = lax.broadcasted_iota(jnp.int32, (RANK, RANK), 0) == lax.broadcasted_iota(
        jnp.int32, (RANK, RANK), 1
    )
    work[:, RANK:] = eye.astype(F32)
    arrived(gg.at[:, 1 - c], i_gc)
    work[:, 0:RANK] = gg[...].reshape(RANK, RANK)

    panels(0, 1)
    third_sends(0)
    panels(1, 4)
    third_sends(1)
    panels(4, 6)
    own_sums(0)
    gather_w.begin(0)
    panels(6, 8)
    own_sums(1)
    gather_w.begin(1)

    panels(8, 10)
    for d in (1, 3, 2):
        gather_w.middle(0, d)
    panels(10, 12)
    for d in (1, 3, 2):
        gather_w.middle(1, d)
    for keep in keeps:
        keep.wait()
    hand_over(0, 0)
    panels(12, 14)
    gather_w.relay(0, 0)
    panels(14, 16)
    gather_w.relay(1, 0)

    low_inv = work.at[:, pl.ds(RANK, RANK)]
    total = jnp.zeros((1, RANK), F32)
    for s in range(2):
        right = dot_nt(wown[s], low_inv[...], HIGHEST)
        total = total + jnp.sum(right * right, axis=0, keepdims=True)
    i_qx, i_qy, i_qz, i_qc = take(3), take(3), take(3), take(1)
    sx[x] = jnp.broadcast_to(total, (8, RANK))
    exchange(sx, x, lambda to: dev(to, y, c, z), i_qx)
    gather_w.relay(0, 3)
    gather_w.relay(1, 3)
    q_s[...] = dot_nt(jnp.transpose(p_own[...]), low_inv[...], HIGHEST)
    sy[y] = exchanged(sx, x, i_qx)
    exchange(sy, y, lambda to: dev(x, to, c, z), i_qy)
    gather_w.relay(0, 1)
    gather_w.relay(1, 1)
    lhs_out[0:ROWS, :] = (-0.05 * dot(q_s[...], low_inv[...], HIGHEST)).astype(BF16)
    sz[z] = exchanged(sy, y, i_qy)
    exchange(sz, z, lambda to: dev(x, y, c, to), i_qz)
    gather_w.relay(0, 2)
    gather_w.relay(1, 2)
    hand_over(1, -1)
    hand_over(2, 1)
    sc[c] = exchanged(sz, z, i_qz)
    start(sc.at[c], sc.at[c], sib, i_qc)
    arrived(sc.at[1 - c], i_qc)
    norm = 1.0 / (jnp.sqrt((sc[0] + sc[1])[0:1, :]) + 1e-06)
    unit_scale = (M_ROWS * N_COLS / RANK) ** 0.5
    high, low = split(dot(q_s[...] * (unit_scale * norm), low_inv[...], HIGHEST))
    lhs_out[ROWS : 2 * ROWS, :] = low
    lhs_out[2 * ROWS + 16 : 3 * ROWS + 16, :] = high
    pick = lax.broadcasted_iota(jnp.int32, (16, RANK), 1) == (
        8 * f + lax.broadcasted_iota(jnp.int32, (16, RANK), 0)
    )
    high, low = split(dot(jnp.where(pick, norm, 0.0), low_inv[...], HIGHEST))
    lhs_out[2 * ROWS : 2 * ROWS + 16, :] = low
    lhs_out[3 * ROWS + 16 :, :] = high
    for k in (0, 3, 1, 2):
        for u in range(2):
            gather_w.finish(u, k)
    hand_over(3, 2)
    for n, step in enumerate((0, -1, 1, 2)):
        for s in range(2):
            at = pl.ds(32 * (1 - c) + 16 * s + 4 * mod(ab(s)[0] + step), 4)
            arrived(wt_out.at[at], i_w + 2 * n + s)
    sent()

def reduce_right(momentum, gradient, right_prev):
    vmem = pltpu.VMEM
    any_space = pl.BlockSpec(memory_space=pl.ANY)
    in_hbm = pl.BlockSpec(memory_space=pltpu.HBM)
    in_vmem = pl.BlockSpec(memory_space=pltpu.VMEM)
    return pl.pallas_call(
        kernel,
        out_shape=(
            jax.ShapeDtypeStruct((64, PIECE, RANK), F32),
            jax.ShapeDtypeStruct((3 * ROWS + 32, RANK), BF16),
        ),
        in_specs=[in_hbm, in_hbm, in_hbm],
        out_specs=(any_space, in_vmem),
        scratch_shapes=[
            vmem((2, ROWS, HALF), F32),
            vmem((2, ROWS, HALF), BF16),
            vmem((8, COLS), F32),
            vmem((N_CHUNK, CHUNK, ROWS), F32),
            vmem((N_CHUNK, CHUNK, ROWS), F32),
            vmem((HALF, 2 * ROWS), BF16),
            vmem((HALF, 2 * ROWS), BF16),
            vmem((2, 4, 4, 16, STREAM), F32),
            vmem((2, 4, 4, 16, 2 * ROWS), F32),
            vmem((RANK, ROWS), F32),
            vmem((RANK, ROWS), F32),
            vmem((5, RANK, ROWS), F32),
            vmem((RANK, ROWS), F32),
            vmem((2 * ROWS, RANK), BF16),
            vmem((2 * ROWS, RANK), BF16),
            vmem((4, 32, RANK), F32),
            vmem((4, 32, RANK), F32),
            vmem((4, 2, 32, RANK), F32),
            vmem((32, PIECE, RANK), F32),
            vmem((2, 4, PIECE, RANK), F32),
            vmem((2, 2, 4, PIECE, RANK), F32),
            vmem((2, 3, PIECE, RANK), F32),
            vmem((2, PIECE, RANK), F32),
            vmem((RANK, 2 * RANK), F32),
            vmem((4, 8, RANK), F32),
            vmem((4, 8, RANK), F32),
            vmem((4, 8, RANK), F32),
            vmem((2, 8, RANK), F32),
            vmem((ROWS, RANK), F32),
            pltpu.SemaphoreType.DMA((N_SEM,)),
            pltpu.SemaphoreType.DMA((N_SEM,)),
            pltpu.SemaphoreType.DMA((11,)),
        ],
        compiler_params=pltpu.CompilerParams(
            collective_id=0, has_side_effects=True, vmem_limit_bytes=MAIN_MIB * 2**20
        ),
        name="reduce_right",
    )(momentum, gradient, right_prev)

def finish_kernel(m, g, wt, lhs, new_hbm, right_hbm, update_hbm, new, right, update, sems):
    top = 2 * ROWS + 16
    steps = COLS // WIDE

    def copies(j, slot):
        at = pl.ds(pl.multiple_of(j * WIDE, WIDE), WIDE)
        return (
            pltpu.make_async_copy(new.at[slot], new_hbm.at[:, at], sems.at[slot]),
            pltpu.make_async_copy(update.at[slot], update_hbm.at[:, at], sems.at[2 + slot]),
        )

    def step(j, carry):
        slot = lax.rem(j, 2)
        at = pl.ds(pl.multiple_of(j * WIDE, WIDE), WIDE)
        high, low = split(wt[at, :])
        one = dot_nt(lhs[...], high)
        two = dot_nt(lhs[top:, :], low)

        @pl.when(j >= 2)
        def _():
            for copy in copies(j - 2, slot):
                copy.wait()

        new[slot] = m[:, at] + g[:, at].astype(F32) + one[0:ROWS]
        update[slot] = (one[top : top + ROWS] + (one[ROWS : 2 * ROWS] + two[0:ROWS])).astype(BF16)
        right[:, at] = (one[top + ROWS :] + (one[2 * ROWS : top] + two[ROWS:]))[0:8]
        for copy in copies(j, slot):
            copy.start()
        return carry

    lax.fori_loop(0, steps, step, 0)
    last = pltpu.make_async_copy(right, right_hbm, sems.at[4])
    last.start()
    for j in (steps - 2, steps - 1):
        for copy in copies(j, j % 2):
            copy.wait()
    last.wait()

def finish(momentum, gradient, wt, lhs):
    in_vmem = pl.BlockSpec(memory_space=pltpu.VMEM)
    any_space = pl.BlockSpec(memory_space=pl.ANY)
    return pl.pallas_call(
        finish_kernel,
        out_shape=(
            jax.ShapeDtypeStruct((ROWS, COLS), F32),
            jax.ShapeDtypeStruct((8, COLS), F32),
            jax.ShapeDtypeStruct((ROWS, COLS), BF16),
        ),
        in_specs=[in_vmem] * 4,
        out_specs=(any_space,) * 3,
        scratch_shapes=[
            pltpu.VMEM((2, ROWS, WIDE), F32),
            pltpu.VMEM((8, COLS), F32),
            pltpu.VMEM((2, ROWS, WIDE), BF16),
            pltpu.SemaphoreType.DMA((5,)),
        ],
        compiler_params=pltpu.CompilerParams(vmem_limit_bytes=FINISH_MIB * 2**20),
        name="finish",
    )(momentum, gradient, wt, lhs)

def on_device(momentum, gradient, right_prev):
    wt, lhs = reduce_right(momentum, gradient, right_prev)
    return finish(momentum, gradient, wt.reshape(COLS, RANK), lhs)

def solution(mesh):
    spec = P("fsdp", "tensor")
    return jax.shard_map(
        on_device, mesh=mesh, in_specs=(spec,) * 3, out_specs=(spec,) * 3, check_vma=False
    )
```

```python
import jax
import jax.numpy as jnp
from jax import lax
from jax.experimental import pallas as pl
from jax.experimental.pallas import tpu as pltpu
from jax.sharding import PartitionSpec as P

M_ROWS = 8192
N_COLS = 26624
RANK = 256
F32 = jnp.float32
BF16 = jnp.bfloat16
MESH = pl.DeviceIdType.MESH
HIGHEST = lax.Precision.HIGHEST

ROWS = 256
COLS = 6656
HALF = COLS // 2
STREAM = HALF // 2
PIECE = STREAM // 16
V_SUB = ((0, 896), (896, STREAM - 896))
W_SUB = ((0, 56), (56, 48))
W_HALF = (((0, 32), (32, 24)), ((56, 24), (80, 24)))
MAIN_MIB = 42
FINISH_MIB = 22
WIDE = 1664
BLOCK = 16
CHUNK = 256
N_CHUNK = HALF // CHUNK
N_SEM = 288

def split(a):
    high = a.astype(BF16)
    return high, (a - high.astype(F32)).astype(BF16)

def dot(a, b, precision=None):
    return jnp.dot(a, b, precision=precision, preferred_element_type=F32)

def dot_nt(a, b, precision=None):
    return lax.dot_general(
        a, b, (((1,), (1,)), ((), ())), precision=precision, preferred_element_type=F32
    )

def dot_tn(a, b, precision=None):
    return lax.dot_general(
        a, b, (((0,), (0,)), ((), ())), precision=precision, preferred_element_type=F32
    )

def row_of(v, i):
    return jnp.broadcast_to(v[i : i + 1, :], v.shape)

def thirds(a):
    one = a.astype(BF16).astype(F32)
    rest = a - one
    two = rest.astype(BF16).astype(F32)
    return one, two, rest - two

def outer(left, right):
    l1, l2, l3 = thirds(left)
    r1, r2, r3 = thirds(right)
    a = jnp.concatenate([l1, l1, l2, l1, l2, l3], axis=0).astype(BF16)
    b = jnp.concatenate([r1, r2, r1, r3, r2, r1], axis=0).astype(BF16)
    return dot_tn(a, b)

def factor_panel(work, base, panel):
    first = base + BLOCK * panel
    sub = lax.broadcasted_iota(jnp.int32, (BLOCK, 128), 0)
    lane = lax.broadcasted_iota(jnp.int32, (BLOCK, 128), 1)
    rows = pl.ds(pl.multiple_of(first, BLOCK), BLOCK)
    parts = [work[rows, 128 * t : 128 * t + 128] for t in range(4)]
    here = pltpu.roll(parts[base // 128], lax.rem(128 - BLOCK * panel, 128), 1)
    cols = [jnp.broadcast_to(here[:, i : i + 1], (BLOCK, 128)) for i in range(BLOCK)]
    for i in range(BLOCK):
        inv = lax.rsqrt(row_of(cols[i], i))
        coef = jnp.where(sub > i, cols[i] * inv, 0.0)
        for t in range(4):
            scaled = row_of(parts[t], i) * inv
            parts[t] = jnp.where(sub == i, scaled, parts[t] - coef * scaled)
        for j in range(i + 1, BLOCK):
            cols[j] = cols[j] - coef * (row_of(cols[j], i) * inv)
    for t in range(4):
        work[rows, 128 * t : 128 * t + 128] = parts[t]
    left = jnp.where(lane > BLOCK * panel + BLOCK - 1, parts[base // 128], 0.0)
    whole = jnp.concatenate(parts, axis=1)
    work[base : base + 128, :] = work[base : base + 128, :] - outer(left, whole)

def kernel(
    m_hbm, g_hbm, v_hbm, wt_out, lhs_out,
    m_v, g_v, v_in, bts, btr, bh, bl, vb, pt, pst, ptr, zr, pts, ph, plo,
    gx, gy, gg, wt, r1, r2, r3, wown, work, sx, sy, sz, sc, q_s,
    ss, rs, ls,
):
    f = lax.axis_index("fsdp")
    z = lax.axis_index("tensor")
    x, y, c = f // 8, lax.rem(f // 2, 4), lax.rem(f, 2)

    def mod(i):
        return lax.rem(i + 8, 4)

    def dev(xx, yy, cc, zz):
        return (mod(xx) * 8 + mod(yy) * 2 + cc, mod(zz))

    sib = dev(x, y, 1 - c, z)
    n_used = [0]

    def take(n):
        at = n_used[0]
        n_used[0] += n
        assert n_used[0] <= N_SEM
        return at

    def send(src, dst, to, i):
        return pltpu.make_async_remote_copy(
            src_ref=src, dst_ref=dst, send_sem=ss.at[i], recv_sem=rs.at[i],
            device_id=to, device_id_type=MESH,
        )

    pending = []

    def start(src, dst, to, i):
        copy = send(src, dst, to, i)
        copy.start()
        pending.append(copy)

    def arrived(dst, i):
        send(dst, dst, sib, i).wait_recv()

    def sent():
        for copy in pending:
            copy.wait_send()
        pending.clear()

    bar = pltpu.get_barrier_semaphore()
    peers = [sib]
    for d in (1, 2, 3):
        peers += [dev(x + d, y, c, z), dev(x, y + d, c, z), dev(x, y, c, z + d)]
    for peer in peers:
        pl.semaphore_signal(bar, inc=1, device_id=peer, device_id_type=MESH)
    v_load = pltpu.make_async_copy(v_hbm, v_in, ls.at[6])
    v_load.start()
    loads = []
    for h in range(2):
        half = (1 - c) if h == 0 else c
        at = pl.ds(pl.multiple_of(half * HALF, 128), HALF)
        loads.append(pltpu.make_async_copy(m_hbm.at[:, at], m_v.at[h], ls.at[2 * h]))
        loads.append(pltpu.make_async_copy(g_hbm.at[:, at], g_v.at[h], ls.at[2 * h + 1]))
    for load in loads:
        load.start()
    v_load.wait()
    pl.semaphore_wait(bar, len(peers))

    def ab(s):
        return (x, y) if s == 0 else (y, x)

    def dev_ab(s, a, b):
        return dev(a, b, c, z) if s == 0 else dev(b, a, c, z)

    class Gather:
        def __init__(self, piece, half, own):
            self.piece, self.half, self.own = piece, half, own
            self.small, self.big, self.forward = take(12), take(32), take(32)

        def i_small(self, s, u, d):
            return self.small + 6 * s + 3 * u + d - 1

        def i_big(self, s, u, way, k):
            return self.big + 16 * s + 8 * u + 4 * way + k

        def i_forward(self, s, u, way, k):
            return self.forward + 16 * s + 8 * u + 4 * way + k

        def begin(self, u):
            for s in range(2):
                a, b = ab(s)
                for d in (1, 3, 2):
                    start(self.own(s, u), self.piece(s, a, b, u), dev_ab(s, a, b + d), self.i_small(s, u, d))

        def spread(self, s, u, k, src):
            a, b = ab(s)
            here = self.piece(s, a, mod(b + k), u)
            start(src, here, dev_ab(s, a + 1, b), self.i_big(s, u, 0, k))
            start(src, here, dev_ab(s, a - 1, b), self.i_big(s, u, 1, k))

        def middle(self, u, d):
            for s in range(2):
                a, b = ab(s)
                piece = self.piece(s, a, mod(b - d), u)
                arrived(piece, self.i_small(s, u, d))
                if d == 1:
                    self.spread(s, u, 0, self.own(s, u))
                self.spread(s, u, 4 - d, piece)

        def relay(self, u, k):
            for s in range(2):
                a, b = ab(s)
                bb = mod(b + k)
                for way, step in ((0, 1), (1, -1)):
                    arrived(self.piece(s, mod(a - step), bb, u), self.i_big(s, u, way, k))
                    part = self.half(s, mod(a - step), bb, u, way)
                    start(part, part, dev_ab(s, a + step, b), self.i_forward(s, u, way, k))

        def finish(self, u, k):
            for s in range(2):
                a, b = ab(s)
                for way in range(2):
                    arrived(self.half(s, mod(a + 2), mod(b + k), u, way), self.i_forward(s, u, way, k))

    i_v = take(2)
    for s in range(2):
        theirs = pl.ds(pl.multiple_of((1 - c) * HALF + s * STREAM, 128), STREAM)
        start(v_in.at[:, theirs], vb.at[s, x, y, pl.ds(8 * c, 8)], sib, i_v + s)
    for s in range(2):
        mine = pl.ds(pl.multiple_of(c * HALF + s * STREAM, 128), STREAM)
        vb[s, x, y, pl.ds(pl.multiple_of(8 * c, 8), 8), :] = v_in[:, mine]
    for s in range(2):
        arrived(vb.at[s, x, y, pl.ds(8 * (1 - c), 8)], i_v + s)

    def v_piece(s, a, b, u):
        at = (s, a, b) if s == 0 else (s, b, a)
        return vb.at[(*at, slice(None), pl.ds(*V_SUB[u]))]

    def v_half(s, a, b, u, h):
        return v_piece(s, a, b, u).at[pl.ds(8 * h, 8)]

    gather_v = Gather(v_piece, v_half, lambda s, u: v_piece(s, *ab(s), u))
    gather_v.begin(0)
    gather_v.begin(1)

    i_b = take(N_CHUNK)
    loads[0].wait()
    loads[1].wait()

    def b_send(j):
        return send(bts.at[j], btr.at[j], sib, i_b + j)

    def other_chunk(j, carry):
        at = pl.ds(pl.multiple_of(j * CHUNK, CHUNK), CHUNK)
        bts[j] = (m_v[0, :, at] + g_v[0, :, at].astype(F32)).T
        b_send(j).start()
        return carry

    def own_chunk(j, carry):
        at = pl.ds(pl.multiple_of(j * CHUNK, CHUNK), CHUNK)
        high, low = split((m_v[1, :, at] + g_v[1, :, at].astype(F32)).T)
        bh[at, 0:ROWS] = high
        bl[at, 0:ROWS] = low
        return carry

    def sibling_chunk(j, carry):
        b_send(j).wait()
        at = pl.ds(pl.multiple_of(j * CHUNK, CHUNK), CHUNK)
        high, low = split(btr[j])
        bh[at, ROWS:] = high
        bl[at, ROWS:] = low
        return carry

    def project(a_of):
        for s in range(2):
            span = slice(s * STREAM, (s + 1) * STREAM)
            a = a_of(ab(s)[0])
            rows = (vb[s, a] if s == 0 else vb[s, :, a]).reshape(64, STREAM)
            high, low = split(rows)
            both = dot(jnp.concatenate([high, low], axis=0), bh[span, :])
            part = (both[0:64] + both[64:] + dot(high, bl[span, :])).reshape(4, 16, 2 * ROWS)
            if s == 0:
                pt[s, a] = part
            else:
                pt[s, :, a] = part

    lax.fori_loop(0, N_CHUNK, other_chunk, 0)
    for d in (1, 3, 2):
        for u in range(2):
            gather_v.middle(u, d)
    loads[2].wait()
    loads[3].wait()
    lax.fori_loop(0, N_CHUNK, own_chunk, 0)
    for u in range(2):
        gather_v.relay(u, 0)
    lax.fori_loop(0, N_CHUNK, sibling_chunk, 0)
    for k in (3, 1):
        for u in range(2):
            gather_v.relay(u, k)
    project(lambda a: a)
    for u in range(2):
        gather_v.relay(u, 2)
    project(lambda a: mod(a - 1))
    project(lambda a: mod(a + 1))
    for k in (0, 3, 1, 2):
        for u in range(2):
            gather_v.finish(u, k)

    project(lambda a: mod(a + 2))
    sent()

    i_p, i_z, i_s = take(4), take(8), take(4)
    parts = [pl.ds(64 * n, 64) for n in range(4)]
    near = z + 1 - 2 * lax.rem(z, 2)
    far = 3 - z
    for n in range(4):
        pst[parts[n], :] = (pt[0, n, :, :, ROWS:] + pt[1, n, :, :, ROWS:]).reshape(64, ROWS)
        start(pst.at[parts[n]], ptr.at[parts[n]], sib, i_p + n)
    for n in range(4):
        zr[0, parts[n], :] = (pt[0, n, :, :, 0:ROWS] + pt[1, n, :, :, 0:ROWS]).reshape(64, ROWS)
    for step in range(3):
        for n in range(4):
            at = parts[n]
            if step == 0:
                arrived(ptr.at[at], i_p + n)
                zr[0, at, :] = zr[0, at, :] + ptr[at, :]
            else:
                arrived(zr.at[2 * step - 1, at], i_z + 4 * (step - 1) + n)
                zr[2 * step, at, :] = zr[2 * step - 2, at, :] + zr[2 * step - 1, at, :]
            if step < 2:
                to = near if n % 2 == step else far
                start(zr.at[2 * step, at], zr.at[2 * step + 1, at], dev(x, y, c, to), i_z + 4 * step + n)
            else:
                start(zr.at[4, at], pts.at[at], sib, i_s + n)
    p_own = zr.at[4]
    high, low = split(p_own[...].T)
    ph[0:ROWS, :] = high
    plo[0:ROWS, :] = low
    for n in range(4):
        arrived(pts.at[parts[n]], i_s + n)
    high, low = split(pts[...].T)
    ph[ROWS:, :] = high
    plo[ROWS:, :] = low

    def exchange(slots, at, where, i):
        for d in (1, 2, 3):
            start(slots.at[at], slots.at[at], where(at + d), i + d - 1)

    def exchanged(slots, at, i):
        for d in (1, 2, 3):
            arrived(slots.at[mod(at - d)], i + d - 1)
        return slots[0] + slots[1] + slots[2] + slots[3]

    share = pl.ds(pl.multiple_of(32 * (2 * z + c), 32), 32)
    gx[x] = dot_nt(zr[4, share, :], p_own[...], HIGHEST) + dot_nt(pts[share, :], pts[...], HIGHEST)
    i_gx, i_gy, i_gz, i_gc = take(3), take(3), take(3), take(1)
    exchange(gx, x, lambda to: dev(to, y, c, z), i_gx)

    def right_part(s, a):
        row = pl.multiple_of(s * STREAM + a * 4 * PIECE, 16)
        at = pl.ds(row, 4 * PIECE)
        part = dot(bh[at, :], ph[...]) + dot(bh[at, :], plo[...]) + dot(bl[at, :], ph[...])
        wt[pl.ds(16 * s + 4 * a, 4)] = part.reshape(4, PIECE, RANK)

    i_r1, i_r2, i_r3 = take(8), take(8), take(12)

    def group(s, a):
        return pl.ds(16 * s + 4 * mod(a), 4)

    def first_sends(s):
        a, b = ab(s)
        for u in range(2):
            for way, step in ((0, 1), (1, -1)):
                part = pl.ds(*W_HALF[u][way])
                start(wt.at[group(s, a + 2), part], r1.at[s, :, part], dev_ab(s, a + step, b), i_r1 + 4 * s + 2 * u + way)

    def second_sends(u):
        sub = pl.ds(*W_SUB[u])
        for s in range(2):
            a, b = ab(s)
            for way, step in ((0, 1), (1, -1)):
                part = pl.ds(*W_HALF[u][way])
                arrived(r1.at[s, :, part], i_r1 + 4 * s + 2 * u + way)
                at = group(s, a + step)
                wt[at, part, :] = wt[at, part, :] + r1[s, :, part, :]
                start(wt.at[at, sub], r2.at[s, way, :, sub], dev_ab(s, a + step, b), i_r2 + 4 * s + 2 * u + way)

    def third_sends(u):
        sub = pl.ds(*W_SUB[u])
        for s in range(2):
            a, b = ab(s)
            for way in range(2):
                arrived(r2.at[s, way, :, sub], i_r2 + 4 * s + 2 * u + way)
            here = group(s, a)
            wt[here, sub, :] = wt[here, sub, :] + r2[s, 0, :, sub, :] + r2[s, 1, :, sub, :]
            for d in (1, 3, 2):
                start(wt.at[16 * s + 4 * a + mod(b + d), sub], r3.at[s, d - 1, sub], dev_ab(s, a, b + d), i_r3 + 6 * s + 3 * u + d - 1)

    keeps = []

    def own_sums(u):
        sub = pl.ds(*W_SUB[u])
        for s in range(2):
            a, b = ab(s)
            for d in (1, 3, 2):
                arrived(r3.at[s, d - 1, sub], i_r3 + 6 * s + 3 * u + d - 1)
            own = 16 * s + 4 * a + b
            wown[s, sub, :] = wt[own, sub, :] + r3[s, 0, sub, :] + r3[s, 1, sub, :] + r3[s, 2, sub, :]
            keep = pltpu.make_async_copy(wown.at[s, sub], wt_out.at[32 * c + own, sub], ls.at[7 + 2 * s + u])
            keep.start()
            keeps.append(keep)

    def w_piece(s, a, b, u):
        return wt_out.at[32 * c + 16 * s + 4 * a + b, pl.ds(*W_SUB[u])]

    def w_half(s, a, b, u, h):
        return wt_out.at[32 * c + 16 * s + 4 * a + b, pl.ds(*W_HALF[u][h])]

    gather_w = Gather(w_piece, w_half, lambda s, u: wown.at[s, pl.ds(*W_SUB[u])])
    i_w = take(14)

    def hand_over(n, step):
        for s in range(2):
            at = wt_out.at[pl.ds(32 * c + 16 * s + 4 * mod(ab(s)[0] + step), 4)]
            start(at, at, sib, i_w + 2 * n + s)

    def panels(low, high):
        def one(base):
            def body(p, carry):
                factor_panel(work, base, p)
                return carry

            return body

        per = 128 // BLOCK
        if low < per:
            lax.fori_loop(low, min(high, per), one(0), 0)
        if low < per <= high:
            work[128:, :] = work[128:, :] - dot_tn(work[0:128, 128:256], work[0:128, :], HIGHEST)
        if high > per:
            lax.fori_loop(max(low, per) - per, high - per, one(128), 0)

    for s in range(2):
        right_part(s, mod(ab(s)[0] + 2))
        first_sends(s)
    for s in range(2):
        right_part(s, mod(ab(s)[0] + 1))
        right_part(s, mod(ab(s)[0] - 1))
    gy[y] = exchanged(gx, x, i_gx)
    exchange(gy, y, lambda to: dev(x, to, c, z), i_gy)
    for s in range(2):
        right_part(s, ab(s)[0])
    second_sends(0)
    gg[z, c] = exchanged(gy, y, i_gy)
    for d in (1, 2, 3):
        start(gg.at[z, c], gg.at[z, c], dev(x, y, c, z + d), i_gz + d - 1)
    second_sends(1)
    for d in (1, 2, 3):
        arrived(gg.at[mod(z - d), c], i_gz + d - 1)
    start(gg.at[:, c], gg.at[:, c], sib, i_gc)
    eye = lax.broadcasted_iota(jnp.int32, (RANK, RANK), 0) == lax.broadcasted_iota(
        jnp.int32, (RANK, RANK), 1
    )
    work[:, RANK:] = eye.astype(F32)
    arrived(gg.at[:, 1 - c], i_gc)
    work[:, 0:RANK] = gg[...].reshape(RANK, RANK)

    panels(0, 2)
    third_sends(0)
    panels(2, 5)
    third_sends(1)
    panels(5, 8)
    own_sums(0)
    gather_w.begin(0)
    panels(8, 11)
    own_sums(1)
    gather_w.begin(1)
    panels(11, 13)
    for d in (1, 3, 2):
        gather_w.middle(0, d)
    panels(13, 15)
    for d in (1, 3, 2):
        gather_w.middle(1, d)
    for keep in keeps:
        keep.wait()
    hand_over(0, 0)
    panels(15, 16)

    low_inv = work.at[:, pl.ds(RANK, RANK)]
    total = jnp.zeros((1, RANK), F32)
    for s in range(2):
        right = dot_nt(wown[s], low_inv[...], HIGHEST)
        total = total + jnp.sum(right * right, axis=0, keepdims=True)
    i_qx, i_qy, i_qz, i_qc = take(3), take(3), take(3), take(1)
    sx[x] = jnp.broadcast_to(total, (8, RANK))
    exchange(sx, x, lambda to: dev(to, y, c, z), i_qx)
    gather_w.relay(0, 0)
    gather_w.relay(1, 0)
    gather_w.relay(0, 3)
    gather_w.relay(1, 3)
    sy[y] = exchanged(sx, x, i_qx)
    exchange(sy, y, lambda to: dev(x, to, c, z), i_qy)
    gather_w.relay(0, 1)
    gather_w.relay(1, 1)
    gather_w.relay(0, 2)
    gather_w.relay(1, 2)
    hand_over(1, -1)
    hand_over(2, 1)
    sz[z] = exchanged(sy, y, i_qy)
    exchange(sz, z, lambda to: dev(x, y, c, to), i_qz)
    q_s[...] = dot_nt(jnp.transpose(p_own[...]), low_inv[...], HIGHEST)
    lhs_out[0:ROWS, :] = (-0.05 * dot(q_s[...], low_inv[...], HIGHEST)).astype(BF16)

    def finish_piece(k):
        for u in range(2):
            gather_w.finish(u, k)
        for s in range(2):
            a, b = ab(s)
            at = wt_out.at[32 * c + 16 * s + 4 * mod(a + 2) + mod(b + k)]
            start(at, at, sib, i_w + 6 + 4 * s + k)

    finish_piece(0)
    finish_piece(3)
    sc[c] = exchanged(sz, z, i_qz)
    start(sc.at[c], sc.at[c], sib, i_qc)
    finish_piece(1)
    finish_piece(2)
    arrived(sc.at[1 - c], i_qc)
    norm = 1.0 / (jnp.sqrt((sc[0] + sc[1])[0:1, :]) + 1e-06)
    unit_scale = (M_ROWS * N_COLS / RANK) ** 0.5
    high, low = split(dot(q_s[...] * (unit_scale * norm), low_inv[...], HIGHEST))
    lhs_out[ROWS : 2 * ROWS, :] = low
    lhs_out[2 * ROWS + 16 : 3 * ROWS + 16, :] = high
    pick = lax.broadcasted_iota(jnp.int32, (16, RANK), 1) == (
        8 * f + lax.broadcasted_iota(jnp.int32, (16, RANK), 0)
    )
    high, low = split(dot(jnp.where(pick, norm, 0.0), low_inv[...], HIGHEST))
    lhs_out[2 * ROWS : 2 * ROWS + 16, :] = low
    lhs_out[3 * ROWS + 16 :, :] = high
    for s in range(2):
        a, b = ab(s)
        for n, step in enumerate((0, -1, 1)):
            at = pl.ds(32 * (1 - c) + 16 * s + 4 * mod(a + step), 4)
            arrived(wt_out.at[at], i_w + 2 * n + s)
        for k in range(4):
            at = 32 * (1 - c) + 16 * s + 4 * mod(a + 2) + mod(b + k)
            arrived(wt_out.at[at], i_w + 6 + 4 * s + k)
    sent()

def reduce_right(momentum, gradient, right_prev):
    vmem = pltpu.VMEM
    any_space = pl.BlockSpec(memory_space=pl.ANY)
    in_hbm = pl.BlockSpec(memory_space=pltpu.HBM)
    in_vmem = pl.BlockSpec(memory_space=pltpu.VMEM)
    return pl.pallas_call(
        kernel,
        out_shape=(
            jax.ShapeDtypeStruct((64, PIECE, RANK), F32),
            jax.ShapeDtypeStruct((3 * ROWS + 32, RANK), BF16),
        ),
        in_specs=[in_hbm, in_hbm, in_hbm],
        out_specs=(any_space, in_vmem),
        scratch_shapes=[
            vmem((2, ROWS, HALF), F32),
            vmem((2, ROWS, HALF), BF16),
            vmem((8, COLS), F32),
            vmem((N_CHUNK, CHUNK, ROWS), F32),
            vmem((N_CHUNK, CHUNK, ROWS), F32),
            vmem((HALF, 2 * ROWS), BF16),
            vmem((HALF, 2 * ROWS), BF16),
            vmem((2, 4, 4, 16, STREAM), F32),
            vmem((2, 4, 4, 16, 2 * ROWS), F32),
            vmem((RANK, ROWS), F32),
            vmem((RANK, ROWS), F32),
            vmem((5, RANK, ROWS), F32),
            vmem((RANK, ROWS), F32),
            vmem((2 * ROWS, RANK), BF16),
            vmem((2 * ROWS, RANK), BF16),
            vmem((4, 32, RANK), F32),
            vmem((4, 32, RANK), F32),
            vmem((4, 2, 32, RANK), F32),
            vmem((32, PIECE, RANK), F32),
            vmem((2, 4, PIECE, RANK), F32),
            vmem((2, 2, 4, PIECE, RANK), F32),
            vmem((2, 3, PIECE, RANK), F32),
            vmem((2, PIECE, RANK), F32),
            vmem((RANK, 2 * RANK), F32),
            vmem((4, 8, RANK), F32),
            vmem((4, 8, RANK), F32),
            vmem((4, 8, RANK), F32),
            vmem((2, 8, RANK), F32),
            vmem((ROWS, RANK), F32),
            pltpu.SemaphoreType.DMA((N_SEM,)),
            pltpu.SemaphoreType.DMA((N_SEM,)),
            pltpu.SemaphoreType.DMA((11,)),
        ],
        compiler_params=pltpu.CompilerParams(
            collective_id=0, has_side_effects=True, vmem_limit_bytes=MAIN_MIB * 2**20
        ),
        name="reduce_right",
    )(momentum, gradient, right_prev)

def finish_kernel(m, g, wt, lhs, new_hbm, right_hbm, update_hbm, new, right, update, sems):
    top = 2 * ROWS + 16
    steps = COLS // WIDE

    def copies(j, slot):
        at = pl.ds(pl.multiple_of(j * WIDE, WIDE), WIDE)
        return (
            pltpu.make_async_copy(new.at[slot], new_hbm.at[:, at], sems.at[slot]),
            pltpu.make_async_copy(update.at[slot], update_hbm.at[:, at], sems.at[2 + slot]),
        )

    def step(j, carry):
        slot = lax.rem(j, 2)
        at = pl.ds(pl.multiple_of(j * WIDE, WIDE), WIDE)
        high, low = split(wt[at, :])
        one = dot_nt(lhs[...], high)
        two = dot_nt(lhs[top:, :], low)

        @pl.when(j >= 2)
        def _():
            for copy in copies(j - 2, slot):
                copy.wait()

        new[slot] = m[:, at] + g[:, at].astype(F32) + one[0:ROWS]
        update[slot] = (one[top : top + ROWS] + (one[ROWS : 2 * ROWS] + two[0:ROWS])).astype(BF16)
        right[:, at] = (one[top + ROWS :] + (one[2 * ROWS : top] + two[ROWS:]))[0:8]
        for copy in copies(j, slot):
            copy.start()
        return carry

    lax.fori_loop(0, steps, step, 0)
    last = pltpu.make_async_copy(right, right_hbm, sems.at[4])
    last.start()
    for j in (steps - 2, steps - 1):
        for copy in copies(j, j % 2):
            copy.wait()
    last.wait()

def finish(momentum, gradient, wt, lhs):
    in_vmem = pl.BlockSpec(memory_space=pltpu.VMEM)
    any_space = pl.BlockSpec(memory_space=pl.ANY)
    return pl.pallas_call(
        finish_kernel,
        out_shape=(
            jax.ShapeDtypeStruct((ROWS, COLS), F32),
            jax.ShapeDtypeStruct((8, COLS), F32),
            jax.ShapeDtypeStruct((ROWS, COLS), BF16),
        ),
        in_specs=[in_vmem] * 4,
        out_specs=(any_space,) * 3,
        scratch_shapes=[
            pltpu.VMEM((2, ROWS, WIDE), F32),
            pltpu.VMEM((8, COLS), F32),
            pltpu.VMEM((2, ROWS, WIDE), BF16),
            pltpu.SemaphoreType.DMA((5,)),
        ],
        compiler_params=pltpu.CompilerParams(vmem_limit_bytes=FINISH_MIB * 2**20),
        name="finish",
    )(momentum, gradient, wt, lhs)

def on_device(momentum, gradient, right_prev):
    wt, lhs = reduce_right(momentum, gradient, right_prev)
    return finish(momentum, gradient, wt.reshape(COLS, RANK), lhs)

def solution(mesh):
    spec = P("fsdp", "tensor")
    return jax.shard_map(
        on_device, mesh=mesh, in_specs=(spec,) * 3, out_specs=(spec,) * 3, check_vma=False
    )
```

```python
import jax
import jax.numpy as jnp
from jax import lax
from jax.experimental import pallas as pl
from jax.experimental.pallas import tpu as pltpu
from jax.sharding import PartitionSpec as P

M_ROWS = 8192
N_COLS = 26624
RANK = 256
F32 = jnp.float32
BF16 = jnp.bfloat16
MESH = pl.DeviceIdType.MESH
HIGHEST = lax.Precision.HIGHEST

ROWS = 256
COLS = 6656
HALF = COLS // 2
STREAM = HALF // 2
PIECE = STREAM // 16
V_SUB = ((0, 896), (896, STREAM - 896))
W_SUB = ((0, 56), (56, 48))
W_HALF = (((0, 32), (32, 24)), ((56, 24), (80, 24)))
MAIN_MIB = 42
FINISH_MIB = 22
WIDE = 1664
BLOCK = 16
CHUNK = 256
N_CHUNK = HALF // CHUNK
N_SEM = 288

def split(a):
    high = a.astype(BF16)
    return high, (a - high.astype(F32)).astype(BF16)

def dot(a, b, precision=None):
    return jnp.dot(a, b, precision=precision, preferred_element_type=F32)

def dot_nt(a, b, precision=None):
    return lax.dot_general(
        a, b, (((1,), (1,)), ((), ())), precision=precision, preferred_element_type=F32
    )

def dot_tn(a, b, precision=None):
    return lax.dot_general(
        a, b, (((0,), (0,)), ((), ())), precision=precision, preferred_element_type=F32
    )

def row_of(v, i):
    return jnp.broadcast_to(v[i : i + 1, :], v.shape)

def thirds(a):
    one = a.astype(BF16).astype(F32)
    rest = a - one
    two = rest.astype(BF16).astype(F32)
    return one, two, rest - two

def outer(left, right):
    l1, l2, l3 = thirds(left)
    r1, r2, r3 = thirds(right)
    a = jnp.concatenate([l1, l1, l2, l1, l2, l3], axis=0).astype(BF16)
    b = jnp.concatenate([r1, r2, r1, r3, r2, r1], axis=0).astype(BF16)
    return dot_tn(a, b)

def factor_panel(work, base, panel):
    first = base + BLOCK * panel
    sub = lax.broadcasted_iota(jnp.int32, (BLOCK, 128), 0)
    lane = lax.broadcasted_iota(jnp.int32, (BLOCK, 128), 1)
    rows = pl.ds(pl.multiple_of(first, BLOCK), BLOCK)
    parts = [work[rows, 128 * t : 128 * t + 128] for t in range(4)]
    here = pltpu.roll(parts[base // 128], lax.rem(128 - BLOCK * panel, 128), 1)
    cols = [jnp.broadcast_to(here[:, i : i + 1], (BLOCK, 128)) for i in range(BLOCK)]
    for i in range(BLOCK):
        inv = lax.rsqrt(row_of(cols[i], i))
        coef = jnp.where(sub > i, cols[i] * inv, 0.0)
        for t in range(4):
            scaled = row_of(parts[t], i) * inv
            parts[t] = jnp.where(sub == i, scaled, parts[t] - coef * scaled)
        for j in range(i + 1, BLOCK):
            cols[j] = cols[j] - coef * (row_of(cols[j], i) * inv)
    for t in range(4):
        work[rows, 128 * t : 128 * t + 128] = parts[t]
    left = jnp.where(lane > BLOCK * panel + BLOCK - 1, parts[base // 128], 0.0)
    whole = jnp.concatenate(parts, axis=1)
    work[base : base + 128, :] = work[base : base + 128, :] - outer(left, whole)

def kernel(
    m_hbm, g_hbm, v_hbm, wt_out, lhs_out,
    m_v, g_v, v_in, bts, btr, bh, bl, vb, pt, pst, ptr, zr, pts, ph, plo,
    gx, gy, gg, wt, r1, r2, r3, wown, work, sx, sy, sz, sc, q_s,
    ss, rs, ls,
):
    f = lax.axis_index("fsdp")
    z = lax.axis_index("tensor")
    x, y, c = f // 8, lax.rem(f // 2, 4), lax.rem(f, 2)

    def mod(i):
        return lax.rem(i + 8, 4)

    def dev(xx, yy, cc, zz):
        return (mod(xx) * 8 + mod(yy) * 2 + cc, mod(zz))

    sib = dev(x, y, 1 - c, z)
    n_used = [0]

    def take(n):
        at = n_used[0]
        n_used[0] += n
        assert n_used[0] <= N_SEM
        return at

    def send(src, dst, to, i):
        return pltpu.make_async_remote_copy(
            src_ref=src, dst_ref=dst, send_sem=ss.at[i], recv_sem=rs.at[i],
            device_id=to, device_id_type=MESH,
        )

    pending = []

    def start(src, dst, to, i):
        copy = send(src, dst, to, i)
        copy.start()
        pending.append(copy)

    def arrived(dst, i):
        send(dst, dst, sib, i).wait_recv()

    def sent():
        for copy in pending:
            copy.wait_send()
        pending.clear()

    bar = pltpu.get_barrier_semaphore()
    peers = [sib]
    for d in (1, 2, 3):
        peers += [dev(x + d, y, c, z), dev(x, y + d, c, z), dev(x, y, c, z + d)]
    for peer in peers:
        pl.semaphore_signal(bar, inc=1, device_id=peer, device_id_type=MESH)
    v_load = pltpu.make_async_copy(v_hbm, v_in, ls.at[6])
    v_load.start()
    loads = []
    for h in range(2):
        half = (1 - c) if h == 0 else c
        at = pl.ds(pl.multiple_of(half * HALF, 128), HALF)
        loads.append(pltpu.make_async_copy(m_hbm.at[:, at], m_v.at[h], ls.at[2 * h]))
        loads.append(pltpu.make_async_copy(g_hbm.at[:, at], g_v.at[h], ls.at[2 * h + 1]))
    for load in loads:
        load.start()
    v_load.wait()
    pl.semaphore_wait(bar, len(peers))

    def ab(s):
        return (x, y) if s == 0 else (y, x)

    def dev_ab(s, a, b):
        return dev(a, b, c, z) if s == 0 else dev(b, a, c, z)

    class Gather:
        def __init__(self, piece, half, own):
            self.piece, self.half, self.own = piece, half, own
            self.small, self.big, self.forward = take(12), take(32), take(32)

        def i_small(self, s, u, d):
            return self.small + 6 * s + 3 * u + d - 1

        def i_big(self, s, u, way, k):
            return self.big + 16 * s + 8 * u + 4 * way + k

        def i_forward(self, s, u, way, k):
            return self.forward + 16 * s + 8 * u + 4 * way + k

        def begin(self, u):
            for s in range(2):
                a, b = ab(s)
                for d in (1, 3, 2):
                    start(self.own(s, u), self.piece(s, a, b, u), dev_ab(s, a, b + d), self.i_small(s, u, d))

        def spread(self, s, u, k, src):
            a, b = ab(s)
            here = self.piece(s, a, mod(b + k), u)
            start(src, here, dev_ab(s, a + 1, b), self.i_big(s, u, 0, k))
            start(src, here, dev_ab(s, a - 1, b), self.i_big(s, u, 1, k))

        def middle(self, u, d):
            for s in range(2):
                a, b = ab(s)
                piece = self.piece(s, a, mod(b - d), u)
                arrived(piece, self.i_small(s, u, d))
                if d == 1:
                    self.spread(s, u, 0, self.own(s, u))
                self.spread(s, u, 4 - d, piece)

        def relay(self, u, k):
            for s in range(2):
                a, b = ab(s)
                bb = mod(b + k)
                for way, step in ((0, 1), (1, -1)):
                    arrived(self.piece(s, mod(a - step), bb, u), self.i_big(s, u, way, k))
                    part = self.half(s, mod(a - step), bb, u, way)
                    start(part, part, dev_ab(s, a + step, b), self.i_forward(s, u, way, k))

        def finish(self, u, k):
            for s in range(2):
                a, b = ab(s)
                for way in range(2):
                    arrived(self.half(s, mod(a + 2), mod(b + k), u, way), self.i_forward(s, u, way, k))

    i_v = take(2)
    for s in range(2):
        theirs = pl.ds(pl.multiple_of((1 - c) * HALF + s * STREAM, 128), STREAM)
        start(v_in.at[:, theirs], vb.at[s, x, y, pl.ds(8 * c, 8)], sib, i_v + s)
    for s in range(2):
        mine = pl.ds(pl.multiple_of(c * HALF + s * STREAM, 128), STREAM)
        vb[s, x, y, pl.ds(pl.multiple_of(8 * c, 8), 8), :] = v_in[:, mine]
    for s in range(2):
        arrived(vb.at[s, x, y, pl.ds(8 * (1 - c), 8)], i_v + s)

    def v_piece(s, a, b, u):
        at = (s, a, b) if s == 0 else (s, b, a)
        return vb.at[(*at, slice(None), pl.ds(*V_SUB[u]))]

    def v_half(s, a, b, u, h):
        return v_piece(s, a, b, u).at[pl.ds(8 * h, 8)]

    gather_v = Gather(v_piece, v_half, lambda s, u: v_piece(s, *ab(s), u))
    gather_v.begin(0)
    gather_v.begin(1)

    i_b = take(N_CHUNK)
    loads[0].wait()
    loads[1].wait()

    def b_send(j):
        return send(bts.at[j], btr.at[j], sib, i_b + j)

    def other_chunk(j, carry):
        at = pl.ds(pl.multiple_of(j * CHUNK, CHUNK), CHUNK)
        bts[j] = (m_v[0, :, at] + g_v[0, :, at].astype(F32)).T
        b_send(j).start()
        return carry

    def own_chunk(j, carry):
        at = pl.ds(pl.multiple_of(j * CHUNK, CHUNK), CHUNK)
        high, low = split((m_v[1, :, at] + g_v[1, :, at].astype(F32)).T)
        bh[at, 0:ROWS] = high
        bl[at, 0:ROWS] = low
        return carry

    def sibling_chunk(j, carry):
        b_send(j).wait()
        at = pl.ds(pl.multiple_of(j * CHUNK, CHUNK), CHUNK)
        high, low = split(btr[j])
        bh[at, ROWS:] = high
        bl[at, ROWS:] = low
        return carry

    def project(a_of):
        for s in range(2):
            span = slice(s * STREAM, (s + 1) * STREAM)
            a = a_of(ab(s)[0])
            rows = (vb[s, a] if s == 0 else vb[s, :, a]).reshape(64, STREAM)
            high, low = split(rows)
            both = dot(jnp.concatenate([high, low], axis=0), bh[span, :])
            part = (both[0:64] + both[64:] + dot(high, bl[span, :])).reshape(4, 16, 2 * ROWS)
            if s == 0:
                pt[s, a] = part
            else:
                pt[s, :, a] = part

    lax.fori_loop(0, N_CHUNK, other_chunk, 0)
    for d in (1, 3, 2):
        for u in range(2):
            gather_v.middle(u, d)
    loads[2].wait()
    loads[3].wait()
    lax.fori_loop(0, N_CHUNK, own_chunk, 0)
    for u in range(2):
        gather_v.relay(u, 0)
    lax.fori_loop(0, N_CHUNK, sibling_chunk, 0)
    for k in (3, 1):
        for u in range(2):
            gather_v.relay(u, k)
    project(lambda a: a)
    for u in range(2):
        gather_v.relay(u, 2)
    project(lambda a: mod(a - 1))
    project(lambda a: mod(a + 1))
    for k in (0, 3, 1, 2):
        for u in range(2):
            gather_v.finish(u, k)

    project(lambda a: mod(a + 2))
    sent()

    i_p, i_z, i_s = take(4), take(8), take(4)
    parts = [pl.ds(64 * n, 64) for n in range(4)]
    near = z + 1 - 2 * lax.rem(z, 2)
    far = 3 - z
    for n in range(4):
        pst[parts[n], :] = (pt[0, n, :, :, ROWS:] + pt[1, n, :, :, ROWS:]).reshape(64, ROWS)
        start(pst.at[parts[n]], ptr.at[parts[n]], sib, i_p + n)
    for n in range(4):
        zr[0, parts[n], :] = (pt[0, n, :, :, 0:ROWS] + pt[1, n, :, :, 0:ROWS]).reshape(64, ROWS)
    for step in range(3):
        for n in range(4):
            at = parts[n]
            if step == 0:
                arrived(ptr.at[at], i_p + n)
                zr[0, at, :] = zr[0, at, :] + ptr[at, :]
            else:
                arrived(zr.at[2 * step - 1, at], i_z + 4 * (step - 1) + n)
                zr[2 * step, at, :] = zr[2 * step - 2, at, :] + zr[2 * step - 1, at, :]
            if step < 2:
                to = near if n % 2 == step else far
                start(zr.at[2 * step, at], zr.at[2 * step + 1, at], dev(x, y, c, to), i_z + 4 * step + n)
            else:
                start(zr.at[4, at], pts.at[at], sib, i_s + n)
    p_own = zr.at[4]
    high, low = split(p_own[...].T)
    ph[0:ROWS, :] = high
    plo[0:ROWS, :] = low
    for n in range(4):
        arrived(pts.at[parts[n]], i_s + n)
    high, low = split(pts[...].T)
    ph[ROWS:, :] = high
    plo[ROWS:, :] = low

    def exchange(slots, at, where, i):
        for d in (1, 2, 3):
            start(slots.at[at], slots.at[at], where(at + d), i + d - 1)

    def exchanged(slots, at, i):
        for d in (1, 2, 3):
            arrived(slots.at[mod(at - d)], i + d - 1)
        return slots[0] + slots[1] + slots[2] + slots[3]

    share = pl.ds(pl.multiple_of(32 * (2 * z + c), 32), 32)
    gx[x] = dot_nt(zr[4, share, :], p_own[...], HIGHEST) + dot_nt(pts[share, :], pts[...], HIGHEST)
    i_gx, i_gy, i_gz, i_gc = take(3), take(3), take(3), take(1)
    exchange(gx, x, lambda to: dev(to, y, c, z), i_gx)

    def right_part(s, a):
        row = pl.multiple_of(s * STREAM + a * 4 * PIECE, 16)
        at = pl.ds(row, 4 * PIECE)
        part = dot(bh[at, :], ph[...]) + dot(bh[at, :], plo[...]) + dot(bl[at, :], ph[...])
        wt[pl.ds(16 * s + 4 * a, 4)] = part.reshape(4, PIECE, RANK)

    i_r1, i_r2, i_r3 = take(8), take(8), take(12)

    def group(s, a):
        return pl.ds(16 * s + 4 * mod(a), 4)

    def first_sends(s):
        a, b = ab(s)
        for u in range(2):
            for way, step in ((0, 1), (1, -1)):
                part = pl.ds(*W_HALF[u][way])
                start(wt.at[group(s, a + 2), part], r1.at[s, :, part], dev_ab(s, a + step, b), i_r1 + 4 * s + 2 * u + way)

    def second_sends(u):
        sub = pl.ds(*W_SUB[u])
        for s in range(2):
            a, b = ab(s)
            for way, step in ((0, 1), (1, -1)):
                part = pl.ds(*W_HALF[u][way])
                arrived(r1.at[s, :, part], i_r1 + 4 * s + 2 * u + way)
                at = group(s, a + step)
                wt[at, part, :] = wt[at, part, :] + r1[s, :, part, :]
                start(wt.at[at, sub], r2.at[s, way, :, sub], dev_ab(s, a + step, b), i_r2 + 4 * s + 2 * u + way)

    def third_sends(u):
        sub = pl.ds(*W_SUB[u])
        for s in range(2):
            a, b = ab(s)
            for way in range(2):
                arrived(r2.at[s, way, :, sub], i_r2 + 4 * s + 2 * u + way)
            here = group(s, a)
            wt[here, sub, :] = wt[here, sub, :] + r2[s, 0, :, sub, :] + r2[s, 1, :, sub, :]
            for d in (1, 3, 2):
                start(wt.at[16 * s + 4 * a + mod(b + d), sub], r3.at[s, d - 1, sub], dev_ab(s, a, b + d), i_r3 + 6 * s + 3 * u + d - 1)

    keeps = []

    def own_sums(u):
        sub = pl.ds(*W_SUB[u])
        for s in range(2):
            a, b = ab(s)
            for d in (1, 3, 2):
                arrived(r3.at[s, d - 1, sub], i_r3 + 6 * s + 3 * u + d - 1)
            own = 16 * s + 4 * a + b
            wown[s, sub, :] = wt[own, sub, :] + r3[s, 0, sub, :] + r3[s, 1, sub, :] + r3[s, 2, sub, :]
            keep = pltpu.make_async_copy(wown.at[s, sub], wt_out.at[32 * c + own, sub], ls.at[7 + 2 * s + u])
            keep.start()
            keeps.append(keep)

    def w_piece(s, a, b, u):
        return wt_out.at[32 * c + 16 * s + 4 * a + b, pl.ds(*W_SUB[u])]

    def w_half(s, a, b, u, h):
        return wt_out.at[32 * c + 16 * s + 4 * a + b, pl.ds(*W_HALF[u][h])]

    gather_w = Gather(w_piece, w_half, lambda s, u: wown.at[s, pl.ds(*W_SUB[u])])
    i_w = take(14)

    def hand_over(n, step):
        for s in range(2):
            at = wt_out.at[pl.ds(32 * c + 16 * s + 4 * mod(ab(s)[0] + step), 4)]
            start(at, at, sib, i_w + 2 * n + s)

    def panels(low, high):
        def one(base):
            def body(p, carry):
                factor_panel(work, base, p)
                return carry

            return body

        per = 128 // BLOCK
        if low < per:
            lax.fori_loop(low, min(high, per), one(0), 0)
        if low < per <= high:
            work[128:, :] = work[128:, :] - dot_tn(work[0:128, 128:256], work[0:128, :], HIGHEST)
        if high > per:
            lax.fori_loop(max(low, per) - per, high - per, one(128), 0)

    for s in range(2):
        right_part(s, mod(ab(s)[0] + 2))
        first_sends(s)
    for s in range(2):
        right_part(s, mod(ab(s)[0] + 1))
        right_part(s, mod(ab(s)[0] - 1))
    gy[y] = exchanged(gx, x, i_gx)
    exchange(gy, y, lambda to: dev(x, to, c, z), i_gy)
    for s in range(2):
        right_part(s, ab(s)[0])
    second_sends(0)
    gg[z, c] = exchanged(gy, y, i_gy)
    for d in (1, 2, 3):
        start(gg.at[z, c], gg.at[z, c], dev(x, y, c, z + d), i_gz + d - 1)
    second_sends(1)
    for d in (1, 2, 3):
        arrived(gg.at[mod(z - d), c], i_gz + d - 1)
    start(gg.at[:, c], gg.at[:, c], sib, i_gc)
    third_sends(0)
    eye = lax.broadcasted_iota(jnp.int32, (RANK, RANK), 0) == lax.broadcasted_iota(
        jnp.int32, (RANK, RANK), 1
    )
    work[:, RANK:] = eye.astype(F32)
    arrived(gg.at[:, 1 - c], i_gc)
    work[:, 0:RANK] = gg[...].reshape(RANK, RANK)

    panels(0, 3)
    third_sends(1)
    panels(3, 8)
    own_sums(0)
    gather_w.begin(0)
    panels(8, 12)
    own_sums(1)
    gather_w.begin(1)
    for d in (1, 3, 2):
        gather_w.middle(0, d)
    panels(12, 16)

    low_inv = work.at[:, pl.ds(RANK, RANK)]
    total = jnp.zeros((1, RANK), F32)
    for s in range(2):
        right = dot_nt(wown[s], low_inv[...], HIGHEST)
        total = total + jnp.sum(right * right, axis=0, keepdims=True)
    i_qx, i_qy, i_qz, i_qc = take(3), take(3), take(3), take(1)
    sx[x] = jnp.broadcast_to(total, (8, RANK))
    exchange(sx, x, lambda to: dev(to, y, c, z), i_qx)
    for d in (1, 3, 2):
        gather_w.middle(1, d)
    for keep in keeps:
        keep.wait()
    hand_over(0, 0)
    gather_w.relay(0, 0)
    gather_w.relay(1, 0)
    gather_w.relay(0, 3)
    gather_w.relay(1, 3)
    sy[y] = exchanged(sx, x, i_qx)
    exchange(sy, y, lambda to: dev(x, to, c, z), i_qy)
    gather_w.relay(0, 1)
    gather_w.relay(1, 1)
    gather_w.relay(0, 2)
    gather_w.relay(1, 2)
    hand_over(1, -1)
    hand_over(2, 1)
    sz[z] = exchanged(sy, y, i_qy)
    exchange(sz, z, lambda to: dev(x, y, c, to), i_qz)
    q_s[...] = dot_nt(jnp.transpose(p_own[...]), low_inv[...], HIGHEST)
    lhs_out[0:ROWS, :] = (-0.05 * dot(q_s[...], low_inv[...], HIGHEST)).astype(BF16)

    def finish_piece(k):
        for u in range(2):
            gather_w.finish(u, k)
        for s in range(2):
            a, b = ab(s)
            at = wt_out.at[32 * c + 16 * s + 4 * mod(a + 2) + mod(b + k)]
            start(at, at, sib, i_w + 6 + 4 * s + k)

    finish_piece(0)
    finish_piece(3)
    sc[c] = exchanged(sz, z, i_qz)
    start(sc.at[c], sc.at[c], sib, i_qc)
    finish_piece(1)
    finish_piece(2)
    arrived(sc.at[1 - c], i_qc)
    norm = 1.0 / (jnp.sqrt((sc[0] + sc[1])[0:1, :]) + 1e-06)
    unit_scale = (M_ROWS * N_COLS / RANK) ** 0.5
    high, low = split(dot(q_s[...] * (unit_scale * norm), low_inv[...], HIGHEST))
    lhs_out[ROWS : 2 * ROWS, :] = low
    lhs_out[2 * ROWS + 16 : 3 * ROWS + 16, :] = high
    pick = lax.broadcasted_iota(jnp.int32, (16, RANK), 1) == (
        8 * f + lax.broadcasted_iota(jnp.int32, (16, RANK), 0)
    )
    high, low = split(dot(jnp.where(pick, norm, 0.0), low_inv[...], HIGHEST))
    lhs_out[2 * ROWS : 2 * ROWS + 16, :] = low
    lhs_out[3 * ROWS + 16 :, :] = high
    for s in range(2):
        a, b = ab(s)
        for n, step in enumerate((0, -1, 1)):
            at = pl.ds(32 * (1 - c) + 16 * s + 4 * mod(a + step), 4)
            arrived(wt_out.at[at], i_w + 2 * n + s)
        for k in range(4):
            at = 32 * (1 - c) + 16 * s + 4 * mod(a + 2) + mod(b + k)
            arrived(wt_out.at[at], i_w + 6 + 4 * s + k)
    sent()

def reduce_right(momentum, gradient, right_prev):
    vmem = pltpu.VMEM
    any_space = pl.BlockSpec(memory_space=pl.ANY)
    in_hbm = pl.BlockSpec(memory_space=pltpu.HBM)
    in_vmem = pl.BlockSpec(memory_space=pltpu.VMEM)
    return pl.pallas_call(
        kernel,
        out_shape=(
            jax.ShapeDtypeStruct((64, PIECE, RANK), F32),
            jax.ShapeDtypeStruct((3 * ROWS + 32, RANK), BF16),
        ),
        in_specs=[in_hbm, in_hbm, in_hbm],
        out_specs=(any_space, in_vmem),
        scratch_shapes=[
            vmem((2, ROWS, HALF), F32),
            vmem((2, ROWS, HALF), BF16),
            vmem((8, COLS), F32),
            vmem((N_CHUNK, CHUNK, ROWS), F32),
            vmem((N_CHUNK, CHUNK, ROWS), F32),
            vmem((HALF, 2 * ROWS), BF16),
            vmem((HALF, 2 * ROWS), BF16),
            vmem((2, 4, 4, 16, STREAM), F32),
            vmem((2, 4, 4, 16, 2 * ROWS), F32),
            vmem((RANK, ROWS), F32),
            vmem((RANK, ROWS), F32),
            vmem((5, RANK, ROWS), F32),
            vmem((RANK, ROWS), F32),
            vmem((2 * ROWS, RANK), BF16),
            vmem((2 * ROWS, RANK), BF16),
            vmem((4, 32, RANK), F32),
            vmem((4, 32, RANK), F32),
            vmem((4, 2, 32, RANK), F32),
            vmem((32, PIECE, RANK), F32),
            vmem((2, 4, PIECE, RANK), F32),
            vmem((2, 2, 4, PIECE, RANK), F32),
            vmem((2, 3, PIECE, RANK), F32),
            vmem((2, PIECE, RANK), F32),
            vmem((RANK, 2 * RANK), F32),
            vmem((4, 8, RANK), F32),
            vmem((4, 8, RANK), F32),
            vmem((4, 8, RANK), F32),
            vmem((2, 8, RANK), F32),
            vmem((ROWS, RANK), F32),
            pltpu.SemaphoreType.DMA((N_SEM,)),
            pltpu.SemaphoreType.DMA((N_SEM,)),
            pltpu.SemaphoreType.DMA((11,)),
        ],
        compiler_params=pltpu.CompilerParams(
            collective_id=0, has_side_effects=True, vmem_limit_bytes=MAIN_MIB * 2**20
        ),
        name="reduce_right",
    )(momentum, gradient, right_prev)

def finish_kernel(m, g, wt, lhs, new_hbm, right_hbm, update_hbm, new, right, update, sems):
    top = 2 * ROWS + 16
    steps = COLS // WIDE

    def copies(j, slot):
        at = pl.ds(j * WIDE, WIDE)
        return (
            pltpu.make_async_copy(new.at[slot], new_hbm.at[:, at], sems.at[slot]),
            pltpu.make_async_copy(update.at[slot], update_hbm.at[:, at], sems.at[2 + slot]),
        )

    def products(j):
        at = slice(j * WIDE, (j + 1) * WIDE)
        high, low = split(wt[at, :])
        return dot_nt(lhs[...], high), dot_nt(lhs[top:, :], low)

    ahead = products(0)
    for j in range(steps):
        slot = j % 2
        at = slice(j * WIDE, (j + 1) * WIDE)
        one, two = ahead
        if j + 1 < steps:
            ahead = products(j + 1)
        if j >= 2:
            for copy in copies(j - 2, slot):
                copy.wait()
        new[slot] = m[:, at] + g[:, at].astype(F32) + one[0:ROWS]
        update[slot] = (one[top : top + ROWS] + (one[ROWS : 2 * ROWS] + two[0:ROWS])).astype(BF16)
        right[:, at] = (one[top + ROWS :] + (one[2 * ROWS : top] + two[ROWS:]))[0:8]
        for copy in copies(j, slot):
            copy.start()
    last = pltpu.make_async_copy(right, right_hbm, sems.at[4])
    last.start()
    for j in (steps - 2, steps - 1):
        for copy in copies(j, j % 2):
            copy.wait()
    last.wait()

def finish(momentum, gradient, wt, lhs):
    in_vmem = pl.BlockSpec(memory_space=pltpu.VMEM)
    any_space = pl.BlockSpec(memory_space=pl.ANY)
    return pl.pallas_call(
        finish_kernel,
        out_shape=(
            jax.ShapeDtypeStruct((ROWS, COLS), F32),
            jax.ShapeDtypeStruct((8, COLS), F32),
            jax.ShapeDtypeStruct((ROWS, COLS), BF16),
        ),
        in_specs=[in_vmem] * 4,
        out_specs=(any_space,) * 3,
        scratch_shapes=[
            pltpu.VMEM((2, ROWS, WIDE), F32),
            pltpu.VMEM((8, COLS), F32),
            pltpu.VMEM((2, ROWS, WIDE), BF16),
            pltpu.SemaphoreType.DMA((5,)),
        ],
        compiler_params=pltpu.CompilerParams(vmem_limit_bytes=FINISH_MIB * 2**20),
        name="finish",
    )(momentum, gradient, wt, lhs)

def on_device(momentum, gradient, right_prev):
    wt, lhs = reduce_right(momentum, gradient, right_prev)
    return finish(momentum, gradient, wt.reshape(COLS, RANK), lhs)

def solution(mesh):
    spec = P("fsdp", "tensor")
    return jax.shard_map(
        on_device, mesh=mesh, in_specs=(spec,) * 3, out_specs=(spec,) * 3, check_vma=False
    )
```

```python
import jax
import jax.numpy as jnp
from jax import lax
from jax.experimental import pallas as pl
from jax.experimental.pallas import tpu as pltpu
from jax.sharding import PartitionSpec as P

M_ROWS = 8192
N_COLS = 26624
RANK = 256
F32 = jnp.float32
BF16 = jnp.bfloat16
MESH = pl.DeviceIdType.MESH
HIGHEST = lax.Precision.HIGHEST

ROWS = 256
COLS = 6656
HALF = COLS // 2
STREAM = HALF // 2
PIECE = STREAM // 16
V_SUB = ((0, 896), (896, STREAM - 896))
W_SUB = ((0, 56), (56, 48))
W_HALF = (((0, 32), (32, 24)), ((56, 24), (80, 24)))
MAIN_MIB = 42
FINISH_MIB = 22
WIDE = 1664
BLOCK = 16
CHUNK = 256
N_CHUNK = HALF // CHUNK
N_SEM = 288

def split(a):
    high = a.astype(BF16)
    return high, (a - high.astype(F32)).astype(BF16)

def dot(a, b, precision=None):
    return jnp.dot(a, b, precision=precision, preferred_element_type=F32)

def dot_nt(a, b, precision=None):
    return lax.dot_general(
        a, b, (((1,), (1,)), ((), ())), precision=precision, preferred_element_type=F32
    )

def dot_tn(a, b, precision=None):
    return lax.dot_general(
        a, b, (((0,), (0,)), ((), ())), precision=precision, preferred_element_type=F32
    )

def row_of(v, i):
    return jnp.broadcast_to(v[i : i + 1, :], v.shape)

def thirds(a):
    one = a.astype(BF16).astype(F32)
    rest = a - one
    two = rest.astype(BF16).astype(F32)
    return one, two, rest - two

def outer(left, right):
    l1, l2, l3 = thirds(left)
    r1, r2, r3 = thirds(right)
    a = jnp.concatenate([l1, l1, l2, l1, l2, l3], axis=0).astype(BF16)
    b = jnp.concatenate([r1, r2, r1, r3, r2, r1], axis=0).astype(BF16)
    return dot_tn(a, b)

def factor_panel(work, base, panel):
    first = base + BLOCK * panel
    sub = lax.broadcasted_iota(jnp.int32, (BLOCK, 128), 0)
    lane = lax.broadcasted_iota(jnp.int32, (BLOCK, 128), 1)
    rows = pl.ds(pl.multiple_of(first, BLOCK), BLOCK)
    parts = [work[rows, 128 * t : 128 * t + 128] for t in range(4)]
    here = pltpu.roll(parts[base // 128], lax.rem(128 - BLOCK * panel, 128), 1)
    cols = [jnp.broadcast_to(here[:, i : i + 1], (BLOCK, 128)) for i in range(BLOCK)]
    for i in range(BLOCK):
        inv = lax.rsqrt(row_of(cols[i], i))
        coef = jnp.where(sub > i, cols[i] * inv, 0.0)
        for t in range(4):
            scaled = row_of(parts[t], i) * inv
            parts[t] = jnp.where(sub == i, scaled, parts[t] - coef * scaled)
        for j in range(i + 1, BLOCK):
            cols[j] = cols[j] - coef * (row_of(cols[j], i) * inv)
    for t in range(4):
        work[rows, 128 * t : 128 * t + 128] = parts[t]
    left = jnp.where(lane > BLOCK * panel + BLOCK - 1, parts[base // 128], 0.0)
    whole = jnp.concatenate(parts, axis=1)
    work[base : base + 128, :] = work[base : base + 128, :] - outer(left, whole)

def kernel(
    m_hbm, g_hbm, v_hbm, wt_out, lhs_out,
    m_v, g_v, v_in, bts, btr, bh, bl, vb, pt, pst, ptr, zr, pts, ph, plo,
    gx, gy, gg, wt, r1, r2, r3, wown, work, sx, sy, sz, sc, q_s,
    ss, rs, ls,
):
    f = lax.axis_index("fsdp")
    z = lax.axis_index("tensor")
    x, y, c = f // 8, lax.rem(f // 2, 4), lax.rem(f, 2)

    def mod(i):
        return lax.rem(i + 8, 4)

    def dev(xx, yy, cc, zz):
        return (mod(xx) * 8 + mod(yy) * 2 + cc, mod(zz))

    sib = dev(x, y, 1 - c, z)
    n_used = [0]

    def take(n):
        at = n_used[0]
        n_used[0] += n
        assert n_used[0] <= N_SEM
        return at

    def send(src, dst, to, i):
        return pltpu.make_async_remote_copy(
            src_ref=src, dst_ref=dst, send_sem=ss.at[i], recv_sem=rs.at[i],
            device_id=to, device_id_type=MESH,
        )

    pending = []

    def start(src, dst, to, i):
        copy = send(src, dst, to, i)
        copy.start()
        pending.append(copy)

    def arrived(dst, i):
        send(dst, dst, sib, i).wait_recv()

    def sent():
        for copy in pending:
            copy.wait_send()
        pending.clear()

    bar = pltpu.get_barrier_semaphore()
    peers = [sib]
    for d in (1, 2, 3):
        peers += [dev(x + d, y, c, z), dev(x, y + d, c, z), dev(x, y, c, z + d)]
    for peer in peers:
        pl.semaphore_signal(bar, inc=1, device_id=peer, device_id_type=MESH)
    v_load = pltpu.make_async_copy(v_hbm, v_in, ls.at[6])
    v_load.start()
    loads = []
    for h in range(2):
        half = (1 - c) if h == 0 else c
        at = pl.ds(pl.multiple_of(half * HALF, 128), HALF)
        loads.append(pltpu.make_async_copy(m_hbm.at[:, at], m_v.at[h], ls.at[2 * h]))
        loads.append(pltpu.make_async_copy(g_hbm.at[:, at], g_v.at[h], ls.at[2 * h + 1]))
    for load in loads:
        load.start()
    v_load.wait()
    pl.semaphore_wait(bar, len(peers))

    def ab(s):
        return (x, y) if s == 0 else (y, x)

    def dev_ab(s, a, b):
        return dev(a, b, c, z) if s == 0 else dev(b, a, c, z)

    class Gather:
        def __init__(self, piece, half, own):
            self.piece, self.half, self.own = piece, half, own
            self.small, self.big, self.forward = take(12), take(32), take(32)

        def i_small(self, s, u, d):
            return self.small + 6 * s + 3 * u + d - 1

        def i_big(self, s, u, way, k):
            return self.big + 16 * s + 8 * u + 4 * way + k

        def i_forward(self, s, u, way, k):
            return self.forward + 16 * s + 8 * u + 4 * way + k

        def begin(self, u):
            for s in range(2):
                a, b = ab(s)
                for d in (1, 3, 2):
                    start(self.own(s, u), self.piece(s, a, b, u), dev_ab(s, a, b + d), self.i_small(s, u, d))

        def spread(self, s, u, k, src):
            a, b = ab(s)
            here = self.piece(s, a, mod(b + k), u)
            start(src, here, dev_ab(s, a + 1, b), self.i_big(s, u, 0, k))
            start(src, here, dev_ab(s, a - 1, b), self.i_big(s, u, 1, k))

        def middle(self, u, d):
            for s in range(2):
                a, b = ab(s)
                piece = self.piece(s, a, mod(b - d), u)
                arrived(piece, self.i_small(s, u, d))
                if d == 1:
                    self.spread(s, u, 0, self.own(s, u))
                self.spread(s, u, 4 - d, piece)

        def relay(self, u, k):
            for s in range(2):
                a, b = ab(s)
                bb = mod(b + k)
                for way, step in ((0, 1), (1, -1)):
                    arrived(self.piece(s, mod(a - step), bb, u), self.i_big(s, u, way, k))
                    part = self.half(s, mod(a - step), bb, u, way)
                    start(part, part, dev_ab(s, a + step, b), self.i_forward(s, u, way, k))

        def finish(self, u, k):
            for s in range(2):
                a, b = ab(s)
                for way in range(2):
                    arrived(self.half(s, mod(a + 2), mod(b + k), u, way), self.i_forward(s, u, way, k))

    i_v = take(2)
    for s in range(2):
        theirs = pl.ds(pl.multiple_of((1 - c) * HALF + s * STREAM, 128), STREAM)
        start(v_in.at[:, theirs], vb.at[s, x, y, pl.ds(8 * c, 8)], sib, i_v + s)
    for s in range(2):
        mine = pl.ds(pl.multiple_of(c * HALF + s * STREAM, 128), STREAM)
        vb[s, x, y, pl.ds(pl.multiple_of(8 * c, 8), 8), :] = v_in[:, mine]
    for s in range(2):
        arrived(vb.at[s, x, y, pl.ds(8 * (1 - c), 8)], i_v + s)

    def v_piece(s, a, b, u):
        at = (s, a, b) if s == 0 else (s, b, a)
        return vb.at[(*at, slice(None), pl.ds(*V_SUB[u]))]

    def v_half(s, a, b, u, h):
        return v_piece(s, a, b, u).at[pl.ds(8 * h, 8)]

    gather_v = Gather(v_piece, v_half, lambda s, u: v_piece(s, *ab(s), u))
    gather_v.begin(0)
    gather_v.begin(1)

    i_b = take(N_CHUNK)
    loads[0].wait()
    loads[1].wait()

    def b_send(j):
        return send(bts.at[j], btr.at[j], sib, i_b + j)

    def other_chunk(j, carry):
        at = pl.ds(pl.multiple_of(j * CHUNK, CHUNK), CHUNK)
        bts[j] = (m_v[0, :, at] + g_v[0, :, at].astype(F32)).T
        b_send(j).start()
        return carry

    def own_chunk(j, carry):
        at = pl.ds(pl.multiple_of(j * CHUNK, CHUNK), CHUNK)
        high, low = split((m_v[1, :, at] + g_v[1, :, at].astype(F32)).T)
        bh[at, 0:ROWS] = high
        bl[at, 0:ROWS] = low
        return carry

    def sibling_chunk(j, carry):
        b_send(j).wait()
        at = pl.ds(pl.multiple_of(j * CHUNK, CHUNK), CHUNK)
        high, low = split(btr[j])
        bh[at, ROWS:] = high
        bl[at, ROWS:] = low
        return carry

    def project(a_of):
        for s in range(2):
            span = slice(s * STREAM, (s + 1) * STREAM)
            a = a_of(ab(s)[0])
            rows = (vb[s, a] if s == 0 else vb[s, :, a]).reshape(64, STREAM)
            high, low = split(rows)
            both = dot(jnp.concatenate([high, low], axis=0), bh[span, :])
            part = (both[0:64] + both[64:] + dot(high, bl[span, :])).reshape(4, 16, 2 * ROWS)
            if s == 0:
                pt[s, a] = part
            else:
                pt[s, :, a] = part

    lax.fori_loop(0, N_CHUNK, other_chunk, 0)
    for d in (1, 3, 2):
        for u in range(2):
            gather_v.middle(u, d)
    loads[2].wait()
    loads[3].wait()
    lax.fori_loop(0, N_CHUNK, own_chunk, 0)
    for u in range(2):
        gather_v.relay(u, 0)
    lax.fori_loop(0, N_CHUNK, sibling_chunk, 0)
    for k in (3, 1):
        for u in range(2):
            gather_v.relay(u, k)
    project(lambda a: a)
    for u in range(2):
        gather_v.relay(u, 2)
    project(lambda a: mod(a - 1))
    project(lambda a: mod(a + 1))
    for k in (0, 3, 1, 2):
        for u in range(2):
            gather_v.finish(u, k)

    project(lambda a: mod(a + 2))
    sent()

    i_p, i_z, i_s = take(4), take(8), take(4)
    parts = [pl.ds(64 * n, 64) for n in range(4)]
    near = z + 1 - 2 * lax.rem(z, 2)
    far = 3 - z
    for n in range(4):
        pst[parts[n], :] = (pt[0, n, :, :, ROWS:] + pt[1, n, :, :, ROWS:]).reshape(64, ROWS)
        start(pst.at[parts[n]], ptr.at[parts[n]], sib, i_p + n)
    for n in range(4):
        zr[0, parts[n], :] = (pt[0, n, :, :, 0:ROWS] + pt[1, n, :, :, 0:ROWS]).reshape(64, ROWS)
    for step in range(3):
        for n in range(4):
            at = parts[n]
            if step == 0:
                arrived(ptr.at[at], i_p + n)
                zr[0, at, :] = zr[0, at, :] + ptr[at, :]
            else:
                arrived(zr.at[2 * step - 1, at], i_z + 4 * (step - 1) + n)
                zr[2 * step, at, :] = zr[2 * step - 2, at, :] + zr[2 * step - 1, at, :]
            if step < 2:
                to = near if n % 2 == step else far
                start(zr.at[2 * step, at], zr.at[2 * step + 1, at], dev(x, y, c, to), i_z + 4 * step + n)
            else:
                start(zr.at[4, at], pts.at[at], sib, i_s + n)
    p_own = zr.at[4]
    high, low = split(p_own[...].T)
    ph[0:ROWS, :] = high
    plo[0:ROWS, :] = low
    for n in range(4):
        arrived(pts.at[parts[n]], i_s + n)
    high, low = split(pts[...].T)
    ph[ROWS:, :] = high
    plo[ROWS:, :] = low

    def exchange(slots, at, where, i):
        for d in (1, 2, 3):
            start(slots.at[at], slots.at[at], where(at + d), i + d - 1)

    def exchanged(slots, at, i):
        for d in (1, 2, 3):
            arrived(slots.at[mod(at - d)], i + d - 1)
        return slots[0] + slots[1] + slots[2] + slots[3]

    share = pl.ds(pl.multiple_of(32 * (2 * z + c), 32), 32)
    gx[x] = dot_nt(zr[4, share, :], p_own[...], HIGHEST) + dot_nt(pts[share, :], pts[...], HIGHEST)
    i_gx, i_gy, i_gz, i_gc = take(3), take(3), take(3), take(1)
    exchange(gx, x, lambda to: dev(to, y, c, z), i_gx)

    def right_part(s, a):
        row = pl.multiple_of(s * STREAM + a * 4 * PIECE, 16)
        at = pl.ds(row, 4 * PIECE)
        part = dot(bh[at, :], ph[...]) + dot(bh[at, :], plo[...]) + dot(bl[at, :], ph[...])
        wt[pl.ds(16 * s + 4 * a, 4)] = part.reshape(4, PIECE, RANK)

    i_r1, i_r2, i_r3 = take(8), take(8), take(12)

    def group(s, a):
        return pl.ds(16 * s + 4 * mod(a), 4)

    def first_sends(s):
        a, b = ab(s)
        for u in range(2):
            for way, step in ((0, 1), (1, -1)):
                part = pl.ds(*W_HALF[u][way])
                start(wt.at[group(s, a + 2), part], r1.at[s, :, part], dev_ab(s, a + step, b), i_r1 + 4 * s + 2 * u + way)

    def second_sends(u):
        sub = pl.ds(*W_SUB[u])
        for s in range(2):
            a, b = ab(s)
            for way, step in ((0, 1), (1, -1)):
                part = pl.ds(*W_HALF[u][way])
                arrived(r1.at[s, :, part], i_r1 + 4 * s + 2 * u + way)
                at = group(s, a + step)
                wt[at, part, :] = wt[at, part, :] + r1[s, :, part, :]
                start(wt.at[at, sub], r2.at[s, way, :, sub], dev_ab(s, a + step, b), i_r2 + 4 * s + 2 * u + way)

    def third_sends(u):
        sub = pl.ds(*W_SUB[u])
        for s in range(2):
            a, b = ab(s)
            for way in range(2):
                arrived(r2.at[s, way, :, sub], i_r2 + 4 * s + 2 * u + way)
            here = group(s, a)
            wt[here, sub, :] = wt[here, sub, :] + r2[s, 0, :, sub, :] + r2[s, 1, :, sub, :]
            for d in (1, 3, 2):
                start(wt.at[16 * s + 4 * a + mod(b + d), sub], r3.at[s, d - 1, sub], dev_ab(s, a, b + d), i_r3 + 6 * s + 3 * u + d - 1)

    keeps = []

    def own_sums(u):
        sub = pl.ds(*W_SUB[u])
        for s in range(2):
            a, b = ab(s)
            for d in (1, 3, 2):
                arrived(r3.at[s, d - 1, sub], i_r3 + 6 * s + 3 * u + d - 1)
            own = 16 * s + 4 * a + b
            wown[s, sub, :] = wt[own, sub, :] + r3[s, 0, sub, :] + r3[s, 1, sub, :] + r3[s, 2, sub, :]
            keep = pltpu.make_async_copy(wown.at[s, sub], wt_out.at[32 * c + own, sub], ls.at[7 + 2 * s + u])
            keep.start()
            keeps.append(keep)

    def w_piece(s, a, b, u):
        return wt_out.at[32 * c + 16 * s + 4 * a + b, pl.ds(*W_SUB[u])]

    def w_half(s, a, b, u, h):
        return wt_out.at[32 * c + 16 * s + 4 * a + b, pl.ds(*W_HALF[u][h])]

    gather_w = Gather(w_piece, w_half, lambda s, u: wown.at[s, pl.ds(*W_SUB[u])])
    i_w = take(14)

    def hand_over(n, step):
        for s in range(2):
            at = wt_out.at[pl.ds(32 * c + 16 * s + 4 * mod(ab(s)[0] + step), 4)]
            start(at, at, sib, i_w + 2 * n + s)

    def panels(low, high):
        def one(base):
            def body(p, carry):
                factor_panel(work, base, p)
                return carry

            return body

        per = 128 // BLOCK
        if low < per:
            lax.fori_loop(low, min(high, per), one(0), 0)
        if low < per <= high:
            work[128:, :] = work[128:, :] - dot_tn(work[0:128, 128:256], work[0:128, :], HIGHEST)
        if high > per:
            lax.fori_loop(max(low, per) - per, high - per, one(128), 0)

    for s in range(2):
        right_part(s, mod(ab(s)[0] + 2))
        first_sends(s)
    for s in range(2):
        right_part(s, mod(ab(s)[0] + 1))
        right_part(s, mod(ab(s)[0] - 1))
    gy[y] = exchanged(gx, x, i_gx)
    exchange(gy, y, lambda to: dev(x, to, c, z), i_gy)
    second_sends(0)
    for s in range(2):
        right_part(s, ab(s)[0])
    gg[z, c] = exchanged(gy, y, i_gy)
    for d in (1, 2, 3):
        start(gg.at[z, c], gg.at[z, c], dev(x, y, c, z + d), i_gz + d - 1)
    second_sends(1)
    for d in (1, 2, 3):
        arrived(gg.at[mod(z - d), c], i_gz + d - 1)
    start(gg.at[:, c], gg.at[:, c], sib, i_gc)
    third_sends(0)
    eye = lax.broadcasted_iota(jnp.int32, (RANK, RANK), 0) == lax.broadcasted_iota(
        jnp.int32, (RANK, RANK), 1
    )
    work[:, RANK:] = eye.astype(F32)
    arrived(gg.at[:, 1 - c], i_gc)
    work[:, 0:RANK] = gg[...].reshape(RANK, RANK)

    panels(0, 3)
    third_sends(1)
    panels(3, 8)
    own_sums(0)
    gather_w.begin(0)
    panels(8, 12)
    own_sums(1)
    gather_w.begin(1)
    for d in (1, 3, 2):
        gather_w.middle(0, d)
    panels(12, 16)

    low_inv = work.at[:, pl.ds(RANK, RANK)]
    total = jnp.zeros((1, RANK), F32)
    for s in range(2):
        right = dot_nt(wown[s], low_inv[...], HIGHEST)
        total = total + jnp.sum(right * right, axis=0, keepdims=True)
    i_qx, i_qy, i_qz, i_qc = take(3), take(3), take(3), take(1)
    sx[x] = jnp.broadcast_to(total, (8, RANK))
    exchange(sx, x, lambda to: dev(to, y, c, z), i_qx)
    for d in (1, 3, 2):
        gather_w.middle(1, d)
    for keep in keeps:
        keep.wait()
    hand_over(0, 0)
    gather_w.relay(0, 0)
    gather_w.relay(1, 0)
    gather_w.relay(0, 3)
    gather_w.relay(1, 3)
    sy[y] = exchanged(sx, x, i_qx)
    exchange(sy, y, lambda to: dev(x, to, c, z), i_qy)
    gather_w.relay(0, 1)
    gather_w.relay(1, 1)
    gather_w.relay(0, 2)
    gather_w.relay(1, 2)
    hand_over(1, -1)
    hand_over(2, 1)
    sz[z] = exchanged(sy, y, i_qy)
    exchange(sz, z, lambda to: dev(x, y, c, to), i_qz)
    q_s[...] = dot_nt(jnp.transpose(p_own[...]), low_inv[...], HIGHEST)
    lhs_out[0:ROWS, :] = (-0.05 * dot(q_s[...], low_inv[...], HIGHEST)).astype(BF16)

    def finish_piece(k):
        for u in range(2):
            gather_w.finish(u, k)
        for s in range(2):
            a, b = ab(s)
            at = wt_out.at[32 * c + 16 * s + 4 * mod(a + 2) + mod(b + k)]
            start(at, at, sib, i_w + 6 + 4 * s + k)

    finish_piece(0)
    finish_piece(3)
    sc[c] = exchanged(sz, z, i_qz)
    start(sc.at[c], sc.at[c], sib, i_qc)
    finish_piece(1)
    finish_piece(2)
    arrived(sc.at[1 - c], i_qc)
    norm = 1.0 / (jnp.sqrt((sc[0] + sc[1])[0:1, :]) + 1e-06)
    unit_scale = (M_ROWS * N_COLS / RANK) ** 0.5
    high, low = split(dot(q_s[...] * (unit_scale * norm), low_inv[...], HIGHEST))
    lhs_out[ROWS : 2 * ROWS, :] = low
    lhs_out[2 * ROWS + 16 : 3 * ROWS + 16, :] = high
    pick = lax.broadcasted_iota(jnp.int32, (16, RANK), 1) == (
        8 * f + lax.broadcasted_iota(jnp.int32, (16, RANK), 0)
    )
    high, low = split(dot(jnp.where(pick, norm, 0.0), low_inv[...], HIGHEST))
    lhs_out[2 * ROWS : 2 * ROWS + 16, :] = low
    lhs_out[3 * ROWS + 16 :, :] = high
    for s in range(2):
        a, b = ab(s)
        for n, step in enumerate((0, -1, 1)):
            at = pl.ds(32 * (1 - c) + 16 * s + 4 * mod(a + step), 4)
            arrived(wt_out.at[at], i_w + 2 * n + s)
        for k in range(4):
            at = 32 * (1 - c) + 16 * s + 4 * mod(a + 2) + mod(b + k)
            arrived(wt_out.at[at], i_w + 6 + 4 * s + k)
    sent()

def reduce_right(momentum, gradient, right_prev):
    vmem = pltpu.VMEM
    any_space = pl.BlockSpec(memory_space=pl.ANY)
    in_hbm = pl.BlockSpec(memory_space=pltpu.HBM)
    in_vmem = pl.BlockSpec(memory_space=pltpu.VMEM)
    return pl.pallas_call(
        kernel,
        out_shape=(
            jax.ShapeDtypeStruct((64, PIECE, RANK), F32),
            jax.ShapeDtypeStruct((3 * ROWS + 32, RANK), BF16),
        ),
        in_specs=[in_hbm, in_hbm, in_hbm],
        out_specs=(any_space, in_vmem),
        scratch_shapes=[
            vmem((2, ROWS, HALF), F32),
            vmem((2, ROWS, HALF), BF16),
            vmem((8, COLS), F32),
            vmem((N_CHUNK, CHUNK, ROWS), F32),
            vmem((N_CHUNK, CHUNK, ROWS), F32),
            vmem((HALF, 2 * ROWS), BF16),
            vmem((HALF, 2 * ROWS), BF16),
            vmem((2, 4, 4, 16, STREAM), F32),
            vmem((2, 4, 4, 16, 2 * ROWS), F32),
            vmem((RANK, ROWS), F32),
            vmem((RANK, ROWS), F32),
            vmem((5, RANK, ROWS), F32),
            vmem((RANK, ROWS), F32),
            vmem((2 * ROWS, RANK), BF16),
            vmem((2 * ROWS, RANK), BF16),
            vmem((4, 32, RANK), F32),
            vmem((4, 32, RANK), F32),
            vmem((4, 2, 32, RANK), F32),
            vmem((32, PIECE, RANK), F32),
            vmem((2, 4, PIECE, RANK), F32),
            vmem((2, 2, 4, PIECE, RANK), F32),
            vmem((2, 3, PIECE, RANK), F32),
            vmem((2, PIECE, RANK), F32),
            vmem((RANK, 2 * RANK), F32),
            vmem((4, 8, RANK), F32),
            vmem((4, 8, RANK), F32),
            vmem((4, 8, RANK), F32),
            vmem((2, 8, RANK), F32),
            vmem((ROWS, RANK), F32),
            pltpu.SemaphoreType.DMA((N_SEM,)),
            pltpu.SemaphoreType.DMA((N_SEM,)),
            pltpu.SemaphoreType.DMA((11,)),
        ],
        compiler_params=pltpu.CompilerParams(
            collective_id=0, has_side_effects=True, vmem_limit_bytes=MAIN_MIB * 2**20
        ),
        name="reduce_right",
    )(momentum, gradient, right_prev)

def finish_kernel(m, g, wt, lhs, new_hbm, right_hbm, update_hbm, new, right, update, sems):
    top = 2 * ROWS + 16
    steps = COLS // WIDE

    def copies(j, slot):
        at = pl.ds(j * WIDE, WIDE)
        return (
            pltpu.make_async_copy(new.at[slot], new_hbm.at[:, at], sems.at[slot]),
            pltpu.make_async_copy(update.at[slot], update_hbm.at[:, at], sems.at[2 + slot]),
        )

    def products(j):
        at = slice(j * WIDE, (j + 1) * WIDE)
        high, low = split(wt[at, :])
        return dot_nt(lhs[...], high), dot_nt(lhs[top:, :], low)

    ahead = products(0)
    for j in range(steps):
        slot = j % 2
        at = slice(j * WIDE, (j + 1) * WIDE)
        one, two = ahead
        if j + 1 < steps:
            ahead = products(j + 1)
        if j >= 2:
            for copy in copies(j - 2, slot):
                copy.wait()
        new[slot] = m[:, at] + g[:, at].astype(F32) + one[0:ROWS]
        update[slot] = (one[top : top + ROWS] + (one[ROWS : 2 * ROWS] + two[0:ROWS])).astype(BF16)
        right[:, at] = (one[top + ROWS :] + (one[2 * ROWS : top] + two[ROWS:]))[0:8]
        for copy in copies(j, slot):
            copy.start()
    last = pltpu.make_async_copy(right, right_hbm, sems.at[4])
    last.start()
    for j in (steps - 2, steps - 1):
        for copy in copies(j, j % 2):
            copy.wait()
    last.wait()

def finish(momentum, gradient, wt, lhs):
    in_vmem = pl.BlockSpec(memory_space=pltpu.VMEM)
    any_space = pl.BlockSpec(memory_space=pl.ANY)
    return pl.pallas_call(
        finish_kernel,
        out_shape=(
            jax.ShapeDtypeStruct((ROWS, COLS), F32),
            jax.ShapeDtypeStruct((8, COLS), F32),
            jax.ShapeDtypeStruct((ROWS, COLS), BF16),
        ),
        in_specs=[in_vmem] * 4,
        out_specs=(any_space,) * 3,
        scratch_shapes=[
            pltpu.VMEM((2, ROWS, WIDE), F32),
            pltpu.VMEM((8, COLS), F32),
            pltpu.VMEM((2, ROWS, WIDE), BF16),
            pltpu.SemaphoreType.DMA((5,)),
        ],
        compiler_params=pltpu.CompilerParams(vmem_limit_bytes=FINISH_MIB * 2**20),
        name="finish",
    )(momentum, gradient, wt, lhs)

def on_device(momentum, gradient, right_prev):
    wt, lhs = reduce_right(momentum, gradient, right_prev)
    return finish(momentum, gradient, wt.reshape(COLS, RANK), lhs)

def solution(mesh):
    spec = P("fsdp", "tensor")
    return jax.shard_map(
        on_device, mesh=mesh, in_specs=(spec,) * 3, out_specs=(spec,) * 3, check_vma=False
    )
```

```python
import jax
import jax.numpy as jnp
from jax import lax
from jax.experimental import pallas as pl
from jax.experimental.pallas import tpu as pltpu
from jax.sharding import PartitionSpec as P

M_ROWS = 8192
N_COLS = 26624
RANK = 256
F32 = jnp.float32
BF16 = jnp.bfloat16
MESH = pl.DeviceIdType.MESH
HIGHEST = lax.Precision.HIGHEST

ROWS = 256
COLS = 6656
HALF = COLS // 2
STREAM = HALF // 2
PIECE = STREAM // 16
V_SUB = ((0, 896), (896, STREAM - 896))
W_SUB = ((0, 56), (56, 48))
W_HALF = (((0, 32), (32, 24)), ((56, 24), (80, 24)))
MAIN_MIB = 42
FINISH_MIB = 22
WIDE = 1664
BLOCK = 16
CHUNK = 256
N_CHUNK = HALF // CHUNK
N_SEM = 288

def split(a):
    high = a.astype(BF16)
    return high, (a - high.astype(F32)).astype(BF16)

def dot(a, b, precision=None):
    return jnp.dot(a, b, precision=precision, preferred_element_type=F32)

def dot_nt(a, b, precision=None):
    return lax.dot_general(
        a, b, (((1,), (1,)), ((), ())), precision=precision, preferred_element_type=F32
    )

def dot_tn(a, b, precision=None):
    return lax.dot_general(
        a, b, (((0,), (0,)), ((), ())), precision=precision, preferred_element_type=F32
    )

def row_of(v, i):
    return jnp.broadcast_to(v[i : i + 1, :], v.shape)

def thirds(a):
    one = a.astype(BF16).astype(F32)
    rest = a - one
    two = rest.astype(BF16).astype(F32)
    return one, two, rest - two

def outer(left, right):
    l1, l2, l3 = thirds(left)
    r1, r2, r3 = thirds(right)
    a = jnp.concatenate([l1, l1, l2, l1, l2, l3], axis=0).astype(BF16)
    b = jnp.concatenate([r1, r2, r1, r3, r2, r1], axis=0).astype(BF16)
    return dot_tn(a, b)

def factor_panel(work, base, panel):
    first = base + BLOCK * panel
    sub = lax.broadcasted_iota(jnp.int32, (BLOCK, 128), 0)
    lane = lax.broadcasted_iota(jnp.int32, (BLOCK, 128), 1)
    rows = pl.ds(pl.multiple_of(first, BLOCK), BLOCK)
    parts = [work[rows, 128 * t : 128 * t + 128] for t in range(4)]
    here = pltpu.roll(parts[base // 128], lax.rem(128 - BLOCK * panel, 128), 1)
    cols = [jnp.broadcast_to(here[:, i : i + 1], (BLOCK, 128)) for i in range(BLOCK)]
    for i in range(BLOCK):
        inv = lax.rsqrt(row_of(cols[i], i))
        coef = jnp.where(sub > i, cols[i] * inv, 0.0)
        for t in range(4):
            scaled = row_of(parts[t], i) * inv
            parts[t] = jnp.where(sub == i, scaled, parts[t] - coef * scaled)
        for j in range(i + 1, BLOCK):
            cols[j] = cols[j] - coef * (row_of(cols[j], i) * inv)
    for t in range(4):
        work[rows, 128 * t : 128 * t + 128] = parts[t]
    left = jnp.where(lane > BLOCK * panel + BLOCK - 1, parts[base // 128], 0.0)
    whole = jnp.concatenate(parts, axis=1)
    work[base : base + 128, :] = work[base : base + 128, :] - outer(left, whole)

def kernel(
    m_hbm, g_hbm, v_hbm, wt_out, lhs_out,
    m_v, g_v, v_in, bts, btr, bh, bl, vb, pt, pst, ptr, zr, pts, ph, plo,
    gx, gy, gg, wt, r1, r2, r3, wown, work, sx, sy, sz, sc, q_s,
    ss, rs, ls,
):
    f = lax.axis_index("fsdp")
    z = lax.axis_index("tensor")
    x, y, c = f // 8, lax.rem(f // 2, 4), lax.rem(f, 2)

    def mod(i):
        return lax.rem(i + 8, 4)

    def dev(xx, yy, cc, zz):
        return (mod(xx) * 8 + mod(yy) * 2 + cc, mod(zz))

    sib = dev(x, y, 1 - c, z)
    n_used = [0]

    def take(n):
        at = n_used[0]
        n_used[0] += n
        assert n_used[0] <= N_SEM
        return at

    def send(src, dst, to, i):
        return pltpu.make_async_remote_copy(
            src_ref=src, dst_ref=dst, send_sem=ss.at[i], recv_sem=rs.at[i],
            device_id=to, device_id_type=MESH,
        )

    pending = []

    def start(src, dst, to, i):
        copy = send(src, dst, to, i)
        copy.start()
        pending.append(copy)

    def arrived(dst, i):
        send(dst, dst, sib, i).wait_recv()

    def sent():
        for copy in pending:
            copy.wait_send()
        pending.clear()

    bar = pltpu.get_barrier_semaphore()
    peers = [sib]
    for d in (1, 2, 3):
        peers += [dev(x + d, y, c, z), dev(x, y + d, c, z), dev(x, y, c, z + d)]
    for peer in peers:
        pl.semaphore_signal(bar, inc=1, device_id=peer, device_id_type=MESH)
    v_load = pltpu.make_async_copy(v_hbm, v_in, ls.at[6])
    v_load.start()
    loads = []
    for h in range(2):
        half = (1 - c) if h == 0 else c
        at = pl.ds(pl.multiple_of(half * HALF, 128), HALF)
        loads.append(pltpu.make_async_copy(m_hbm.at[:, at], m_v.at[h], ls.at[2 * h]))
        loads.append(pltpu.make_async_copy(g_hbm.at[:, at], g_v.at[h], ls.at[2 * h + 1]))
    for load in loads:
        load.start()
    v_load.wait()
    pl.semaphore_wait(bar, len(peers))

    def ab(s):
        return (x, y) if s == 0 else (y, x)

    def dev_ab(s, a, b):
        return dev(a, b, c, z) if s == 0 else dev(b, a, c, z)

    class Gather:
        def __init__(self, piece, half, own):
            self.piece, self.half, self.own = piece, half, own
            self.small, self.big, self.forward = take(12), take(32), take(32)

        def i_small(self, s, u, d):
            return self.small + 6 * s + 3 * u + d - 1

        def i_big(self, s, u, way, k):
            return self.big + 16 * s + 8 * u + 4 * way + k

        def i_forward(self, s, u, way, k):
            return self.forward + 16 * s + 8 * u + 4 * way + k

        def begin(self, u):
            for s in range(2):
                a, b = ab(s)
                for d in (1, 3, 2):
                    start(self.own(s, u), self.piece(s, a, b, u), dev_ab(s, a, b + d), self.i_small(s, u, d))

        def spread(self, s, u, k, src):
            a, b = ab(s)
            here = self.piece(s, a, mod(b + k), u)
            start(src, here, dev_ab(s, a + 1, b), self.i_big(s, u, 0, k))
            start(src, here, dev_ab(s, a - 1, b), self.i_big(s, u, 1, k))

        def middle(self, u, d):
            for s in range(2):
                a, b = ab(s)
                piece = self.piece(s, a, mod(b - d), u)
                arrived(piece, self.i_small(s, u, d))
                if d == 1:
                    self.spread(s, u, 0, self.own(s, u))
                self.spread(s, u, 4 - d, piece)

        def relay(self, u, k):
            for s in range(2):
                a, b = ab(s)
                bb = mod(b + k)
                for way, step in ((0, 1), (1, -1)):
                    arrived(self.piece(s, mod(a - step), bb, u), self.i_big(s, u, way, k))
                    part = self.half(s, mod(a - step), bb, u, way)
                    start(part, part, dev_ab(s, a + step, b), self.i_forward(s, u, way, k))

        def finish(self, u, k):
            for s in range(2):
                a, b = ab(s)
                for way in range(2):
                    arrived(self.half(s, mod(a + 2), mod(b + k), u, way), self.i_forward(s, u, way, k))

    i_v = take(2)
    for s in range(2):
        theirs = pl.ds(pl.multiple_of((1 - c) * HALF + s * STREAM, 128), STREAM)
        start(v_in.at[:, theirs], vb.at[s, x, y, pl.ds(8 * c, 8)], sib, i_v + s)
    for s in range(2):
        mine = pl.ds(pl.multiple_of(c * HALF + s * STREAM, 128), STREAM)
        vb[s, x, y, pl.ds(pl.multiple_of(8 * c, 8), 8), :] = v_in[:, mine]
    for s in range(2):
        arrived(vb.at[s, x, y, pl.ds(8 * (1 - c), 8)], i_v + s)

    def v_piece(s, a, b, u):
        at = (s, a, b) if s == 0 else (s, b, a)
        return vb.at[(*at, slice(None), pl.ds(*V_SUB[u]))]

    def v_half(s, a, b, u, h):
        return v_piece(s, a, b, u).at[pl.ds(8 * h, 8)]

    gather_v = Gather(v_piece, v_half, lambda s, u: v_piece(s, *ab(s), u))
    gather_v.begin(0)
    gather_v.begin(1)

    i_b = take(N_CHUNK)
    loads[0].wait()
    loads[1].wait()

    def b_send(j):
        return send(bts.at[j], btr.at[j], sib, i_b + j)

    def other_chunk(j, carry):
        at = pl.ds(pl.multiple_of(j * CHUNK, CHUNK), CHUNK)
        bts[j] = (m_v[0, :, at] + g_v[0, :, at].astype(F32)).T
        b_send(j).start()
        return carry

    def own_chunk(j, carry):
        at = pl.ds(pl.multiple_of(j * CHUNK, CHUNK), CHUNK)
        high, low = split((m_v[1, :, at] + g_v[1, :, at].astype(F32)).T)
        bh[at, 0:ROWS] = high
        bl[at, 0:ROWS] = low
        return carry

    def sibling_chunk(j, carry):
        b_send(j).wait()
        at = pl.ds(pl.multiple_of(j * CHUNK, CHUNK), CHUNK)
        high, low = split(btr[j])
        bh[at, ROWS:] = high
        bl[at, ROWS:] = low
        return carry

    def project(a_of):
        for s in range(2):
            span = slice(s * STREAM, (s + 1) * STREAM)
            a = a_of(ab(s)[0])
            rows = (vb[s, a] if s == 0 else vb[s, :, a]).reshape(64, STREAM)
            high, low = split(rows)
            both = dot(jnp.concatenate([high, low], axis=0), bh[span, :])
            part = (both[0:64] + both[64:] + dot(high, bl[span, :])).reshape(4, 16, 2 * ROWS)
            if s == 0:
                pt[s, a] = part
            else:
                pt[s, :, a] = part

    lax.fori_loop(0, N_CHUNK, other_chunk, 0)
    for d in (1, 3, 2):
        for u in range(2):
            gather_v.middle(u, d)
    loads[2].wait()
    loads[3].wait()
    lax.fori_loop(0, N_CHUNK, own_chunk, 0)
    for u in range(2):
        gather_v.relay(u, 0)
    lax.fori_loop(0, N_CHUNK, sibling_chunk, 0)
    for k in (3, 1):
        for u in range(2):
            gather_v.relay(u, k)
    project(lambda a: a)
    for u in range(2):
        gather_v.relay(u, 2)
    project(lambda a: mod(a - 1))
    project(lambda a: mod(a + 1))
    for k in (0, 3, 1, 2):
        for u in range(2):
            gather_v.finish(u, k)

    project(lambda a: mod(a + 2))
    sent()

    i_p, i_z, i_s = take(4), take(8), take(4)
    parts = [pl.ds(64 * n, 64) for n in range(4)]
    near = z + 1 - 2 * lax.rem(z, 2)
    far = 3 - z
    for n in range(4):
        pst[parts[n], :] = (pt[0, n, :, :, ROWS:] + pt[1, n, :, :, ROWS:]).reshape(64, ROWS)
        start(pst.at[parts[n]], ptr.at[parts[n]], sib, i_p + n)
    for n in range(4):
        zr[0, parts[n], :] = (pt[0, n, :, :, 0:ROWS] + pt[1, n, :, :, 0:ROWS]).reshape(64, ROWS)
    for step in range(3):
        for n in range(4):
            at = parts[n]
            if step == 0:
                arrived(ptr.at[at], i_p + n)
                zr[0, at, :] = zr[0, at, :] + ptr[at, :]
            else:
                arrived(zr.at[2 * step - 1, at], i_z + 4 * (step - 1) + n)
                zr[2 * step, at, :] = zr[2 * step - 2, at, :] + zr[2 * step - 1, at, :]
            if step < 2:
                to = near if n % 2 == step else far
                start(zr.at[2 * step, at], zr.at[2 * step + 1, at], dev(x, y, c, to), i_z + 4 * step + n)
            else:
                start(zr.at[4, at], pts.at[at], sib, i_s + n)
    p_own = zr.at[4]
    high, low = split(p_own[...].T)
    ph[0:ROWS, :] = high
    plo[0:ROWS, :] = low
    for n in range(4):
        arrived(pts.at[parts[n]], i_s + n)
    high, low = split(pts[...].T)
    ph[ROWS:, :] = high
    plo[ROWS:, :] = low

    def exchange(slots, at, where, i):
        for d in (1, 2, 3):
            start(slots.at[at], slots.at[at], where(at + d), i + d - 1)

    def exchanged(slots, at, i):
        for d in (1, 2, 3):
            arrived(slots.at[mod(at - d)], i + d - 1)
        return slots[0] + slots[1] + slots[2] + slots[3]

    share = pl.ds(pl.multiple_of(32 * (2 * z + c), 32), 32)
    gx[x] = dot_nt(zr[4, share, :], p_own[...], HIGHEST) + dot_nt(pts[share, :], pts[...], HIGHEST)
    i_gx, i_gy, i_gz, i_gc = take(3), take(3), take(3), take(1)
    exchange(gx, x, lambda to: dev(to, y, c, z), i_gx)

    def right_part(s, a):
        row = pl.multiple_of(s * STREAM + a * 4 * PIECE, 16)
        at = pl.ds(row, 4 * PIECE)
        part = dot(bh[at, :], ph[...]) + dot(bh[at, :], plo[...]) + dot(bl[at, :], ph[...])
        wt[pl.ds(16 * s + 4 * a, 4)] = part.reshape(4, PIECE, RANK)

    i_r1, i_r2, i_r3 = take(8), take(8), take(12)

    def group(s, a):
        return pl.ds(16 * s + 4 * mod(a), 4)

    def first_sends(s):
        a, b = ab(s)
        for u in range(2):
            for way, step in ((0, 1), (1, -1)):
                part = pl.ds(*W_HALF[u][way])
                start(wt.at[group(s, a + 2), part], r1.at[s, :, part], dev_ab(s, a + step, b), i_r1 + 4 * s + 2 * u + way)

    def second_sends(u):
        sub = pl.ds(*W_SUB[u])
        for s in range(2):
            a, b = ab(s)
            for way, step in ((0, 1), (1, -1)):
                part = pl.ds(*W_HALF[u][way])
                arrived(r1.at[s, :, part], i_r1 + 4 * s + 2 * u + way)
                at = group(s, a + step)
                wt[at, part, :] = wt[at, part, :] + r1[s, :, part, :]
                start(wt.at[at, sub], r2.at[s, way, :, sub], dev_ab(s, a + step, b), i_r2 + 4 * s + 2 * u + way)

    def third_sends(u):
        sub = pl.ds(*W_SUB[u])
        for s in range(2):
            a, b = ab(s)
            for way in range(2):
                arrived(r2.at[s, way, :, sub], i_r2 + 4 * s + 2 * u + way)
            here = group(s, a)
            wt[here, sub, :] = wt[here, sub, :] + r2[s, 0, :, sub, :] + r2[s, 1, :, sub, :]
            for d in (1, 3, 2):
                start(wt.at[16 * s + 4 * a + mod(b + d), sub], r3.at[s, d - 1, sub], dev_ab(s, a, b + d), i_r3 + 6 * s + 3 * u + d - 1)

    keeps = []

    def own_sums(u):
        sub = pl.ds(*W_SUB[u])
        for s in range(2):
            a, b = ab(s)
            for d in (1, 3, 2):
                arrived(r3.at[s, d - 1, sub], i_r3 + 6 * s + 3 * u + d - 1)
            own = 16 * s + 4 * a + b
            wown[s, sub, :] = wt[own, sub, :] + r3[s, 0, sub, :] + r3[s, 1, sub, :] + r3[s, 2, sub, :]
            keep = pltpu.make_async_copy(wown.at[s, sub], wt_out.at[32 * c + own, sub], ls.at[7 + 2 * s + u])
            keep.start()
            keeps.append(keep)

    def w_piece(s, a, b, u):
        return wt_out.at[32 * c + 16 * s + 4 * a + b, pl.ds(*W_SUB[u])]

    def w_half(s, a, b, u, h):
        return wt_out.at[32 * c + 16 * s + 4 * a + b, pl.ds(*W_HALF[u][h])]

    gather_w = Gather(w_piece, w_half, lambda s, u: wown.at[s, pl.ds(*W_SUB[u])])
    i_w = take(14)

    def hand_over(n, step):
        for s in range(2):
            at = wt_out.at[pl.ds(32 * c + 16 * s + 4 * mod(ab(s)[0] + step), 4)]
            start(at, at, sib, i_w + 2 * n + s)

    def panels(low, high):
        def one(base):
            def body(p, carry):
                factor_panel(work, base, p)
                return carry

            return body

        per = 128 // BLOCK
        if low < per:
            lax.fori_loop(low, min(high, per), one(0), 0)
        if low < per <= high:
            work[128:, :] = work[128:, :] - dot_tn(work[0:128, 128:256], work[0:128, :], HIGHEST)
        if high > per:
            lax.fori_loop(max(low, per) - per, high - per, one(128), 0)

    for s in range(2):
        right_part(s, mod(ab(s)[0] + 2))
        first_sends(s)
    for s in range(2):
        right_part(s, mod(ab(s)[0] + 1))
        right_part(s, mod(ab(s)[0] - 1))
    gy[y] = exchanged(gx, x, i_gx)
    exchange(gy, y, lambda to: dev(x, to, c, z), i_gy)
    for s in range(2):
        right_part(s, ab(s)[0])
    second_sends(0)
    gg[z, c] = exchanged(gy, y, i_gy)
    for d in (1, 2, 3):
        start(gg.at[z, c], gg.at[z, c], dev(x, y, c, z + d), i_gz + d - 1)
    second_sends(1)
    for d in (1, 2, 3):
        arrived(gg.at[mod(z - d), c], i_gz + d - 1)
    start(gg.at[:, c], gg.at[:, c], sib, i_gc)
    third_sends(0)
    eye = lax.broadcasted_iota(jnp.int32, (RANK, RANK), 0) == lax.broadcasted_iota(
        jnp.int32, (RANK, RANK), 1
    )
    work[:, RANK:] = eye.astype(F32)
    arrived(gg.at[:, 1 - c], i_gc)
    work[:, 0:RANK] = gg[...].reshape(RANK, RANK)

    panels(0, 3)
    third_sends(1)
    panels(3, 8)
    own_sums(0)
    gather_w.begin(0)
    panels(8, 12)
    own_sums(1)
    gather_w.begin(1)
    for d in (1, 3, 2):
        gather_w.middle(0, d)
    panels(12, 16)

    low_inv = work.at[:, pl.ds(RANK, RANK)]
    total = jnp.zeros((1, RANK), F32)
    for s in range(2):
        right = dot_nt(wown[s], low_inv[...], HIGHEST)
        total = total + jnp.sum(right * right, axis=0, keepdims=True)
    i_qx, i_qy, i_qz, i_qc = take(3), take(3), take(3), take(1)
    sx[x] = jnp.broadcast_to(total, (8, RANK))
    exchange(sx, x, lambda to: dev(to, y, c, z), i_qx)
    q_s[...] = dot_nt(jnp.transpose(p_own[...]), low_inv[...], HIGHEST)
    for d in (1, 3, 2):
        gather_w.middle(1, d)
    for keep in keeps:
        keep.wait()
    hand_over(0, 0)
    gather_w.relay(0, 0)
    gather_w.relay(1, 0)
    gather_w.relay(0, 3)
    gather_w.relay(1, 3)
    sy[y] = exchanged(sx, x, i_qx)
    exchange(sy, y, lambda to: dev(x, to, c, z), i_qy)
    lhs_out[0:ROWS, :] = (-0.05 * dot(q_s[...], low_inv[...], HIGHEST)).astype(BF16)
    gather_w.relay(0, 1)
    gather_w.relay(1, 1)
    gather_w.relay(0, 2)
    gather_w.relay(1, 2)
    hand_over(1, -1)
    hand_over(2, 1)
    sz[z] = exchanged(sy, y, i_qy)
    exchange(sz, z, lambda to: dev(x, y, c, to), i_qz)

    def finish_piece(k):
        for u in range(2):
            gather_w.finish(u, k)
        for s in range(2):
            a, b = ab(s)
            at = wt_out.at[32 * c + 16 * s + 4 * mod(a + 2) + mod(b + k)]
            start(at, at, sib, i_w + 6 + 4 * s + k)

    finish_piece(0)
    finish_piece(3)
    sc[c] = exchanged(sz, z, i_qz)
    start(sc.at[c], sc.at[c], sib, i_qc)
    finish_piece(1)
    finish_piece(2)
    arrived(sc.at[1 - c], i_qc)
    norm = 1.0 / (jnp.sqrt((sc[0] + sc[1])[0:1, :]) + 1e-06)
    unit_scale = (M_ROWS * N_COLS / RANK) ** 0.5
    high, low = split(dot(q_s[...] * (unit_scale * norm), low_inv[...], HIGHEST))
    lhs_out[ROWS : 2 * ROWS, :] = low
    lhs_out[2 * ROWS + 16 : 3 * ROWS + 16, :] = high
    pick = lax.broadcasted_iota(jnp.int32, (16, RANK), 1) == (
        8 * f + lax.broadcasted_iota(jnp.int32, (16, RANK), 0)
    )
    high, low = split(dot(jnp.where(pick, norm, 0.0), low_inv[...], HIGHEST))
    lhs_out[2 * ROWS : 2 * ROWS + 16, :] = low
    lhs_out[3 * ROWS + 16 :, :] = high
    for s in range(2):
        a, b = ab(s)
        for n, step in enumerate((0, -1, 1)):
            at = pl.ds(32 * (1 - c) + 16 * s + 4 * mod(a + step), 4)
            arrived(wt_out.at[at], i_w + 2 * n + s)
        for k in range(4):
            at = 32 * (1 - c) + 16 * s + 4 * mod(a + 2) + mod(b + k)
            arrived(wt_out.at[at], i_w + 6 + 4 * s + k)
    sent()

def reduce_right(momentum, gradient, right_prev):
    vmem = pltpu.VMEM
    any_space = pl.BlockSpec(memory_space=pl.ANY)
    in_hbm = pl.BlockSpec(memory_space=pltpu.HBM)
    in_vmem = pl.BlockSpec(memory_space=pltpu.VMEM)
    return pl.pallas_call(
        kernel,
        out_shape=(
            jax.ShapeDtypeStruct((64, PIECE, RANK), F32),
            jax.ShapeDtypeStruct((3 * ROWS + 32, RANK), BF16),
        ),
        in_specs=[in_hbm, in_hbm, in_hbm],
        out_specs=(any_space, in_vmem),
        scratch_shapes=[
            vmem((2, ROWS, HALF), F32),
            vmem((2, ROWS, HALF), BF16),
            vmem((8, COLS), F32),
            vmem((N_CHUNK, CHUNK, ROWS), F32),
            vmem((N_CHUNK, CHUNK, ROWS), F32),
            vmem((HALF, 2 * ROWS), BF16),
            vmem((HALF, 2 * ROWS), BF16),
            vmem((2, 4, 4, 16, STREAM), F32),
            vmem((2, 4, 4, 16, 2 * ROWS), F32),
            vmem((RANK, ROWS), F32),
            vmem((RANK, ROWS), F32),
            vmem((5, RANK, ROWS), F32),
            vmem((RANK, ROWS), F32),
            vmem((2 * ROWS, RANK), BF16),
            vmem((2 * ROWS, RANK), BF16),
            vmem((4, 32, RANK), F32),
            vmem((4, 32, RANK), F32),
            vmem((4, 2, 32, RANK), F32),
            vmem((32, PIECE, RANK), F32),
            vmem((2, 4, PIECE, RANK), F32),
            vmem((2, 2, 4, PIECE, RANK), F32),
            vmem((2, 3, PIECE, RANK), F32),
            vmem((2, PIECE, RANK), F32),
            vmem((RANK, 2 * RANK), F32),
            vmem((4, 8, RANK), F32),
            vmem((4, 8, RANK), F32),
            vmem((4, 8, RANK), F32),
            vmem((2, 8, RANK), F32),
            vmem((ROWS, RANK), F32),
            pltpu.SemaphoreType.DMA((N_SEM,)),
            pltpu.SemaphoreType.DMA((N_SEM,)),
            pltpu.SemaphoreType.DMA((11,)),
        ],
        compiler_params=pltpu.CompilerParams(
            collective_id=0, has_side_effects=True, vmem_limit_bytes=MAIN_MIB * 2**20
        ),
        name="reduce_right",
    )(momentum, gradient, right_prev)

def finish_kernel(m, g, wt, lhs, new_hbm, right_hbm, update_hbm, new, right, update, sems):
    top = 2 * ROWS + 16
    steps = COLS // WIDE

    def copies(j, slot):
        at = pl.ds(j * WIDE, WIDE)
        return (
            pltpu.make_async_copy(new.at[slot], new_hbm.at[:, at], sems.at[slot]),
            pltpu.make_async_copy(update.at[slot], update_hbm.at[:, at], sems.at[2 + slot]),
        )

    def products(j):
        at = slice(j * WIDE, (j + 1) * WIDE)
        high, low = split(wt[at, :])
        return dot_nt(lhs[...], high), dot_nt(lhs[top:, :], low)

    ahead = products(0)
    for j in range(steps):
        slot = j % 2
        at = slice(j * WIDE, (j + 1) * WIDE)
        one, two = ahead
        if j + 1 < steps:
            ahead = products(j + 1)
        if j >= 2:
            for copy in copies(j - 2, slot):
                copy.wait()
        new[slot] = m[:, at] + g[:, at].astype(F32) + one[0:ROWS]
        update[slot] = (one[top : top + ROWS] + (one[ROWS : 2 * ROWS] + two[0:ROWS])).astype(BF16)
        right[:, at] = (one[top + ROWS :] + (one[2 * ROWS : top] + two[ROWS:]))[0:8]
        for copy in copies(j, slot):
            copy.start()
    last = pltpu.make_async_copy(right, right_hbm, sems.at[4])
    last.start()
    for j in (steps - 2, steps - 1):
        for copy in copies(j, j % 2):
            copy.wait()
    last.wait()

def finish(momentum, gradient, wt, lhs):
    in_vmem = pl.BlockSpec(memory_space=pltpu.VMEM)
    any_space = pl.BlockSpec(memory_space=pl.ANY)
    return pl.pallas_call(
        finish_kernel,
        out_shape=(
            jax.ShapeDtypeStruct((ROWS, COLS), F32),
            jax.ShapeDtypeStruct((8, COLS), F32),
            jax.ShapeDtypeStruct((ROWS, COLS), BF16),
        ),
        in_specs=[in_vmem] * 4,
        out_specs=(any_space,) * 3,
        scratch_shapes=[
            pltpu.VMEM((2, ROWS, WIDE), F32),
            pltpu.VMEM((8, COLS), F32),
            pltpu.VMEM((2, ROWS, WIDE), BF16),
            pltpu.SemaphoreType.DMA((5,)),
        ],
        compiler_params=pltpu.CompilerParams(vmem_limit_bytes=FINISH_MIB * 2**20),
        name="finish",
    )(momentum, gradient, wt, lhs)

def on_device(momentum, gradient, right_prev):
    wt, lhs = reduce_right(momentum, gradient, right_prev)
    return finish(momentum, gradient, wt.reshape(COLS, RANK), lhs)

def solution(mesh):
    spec = P("fsdp", "tensor")
    return jax.shard_map(
        on_device, mesh=mesh, in_specs=(spec,) * 3, out_specs=(spec,) * 3, check_vma=False
    )
```
